32 devices in a mesh: dp: 2 (over y), rows: 4 (over z), cols: 4 (over x, core).
Axes of the slice: x: 2, y: 2, z: 4, core: 2. Of those that a mesh axis runs over, the one named last changes fastest.
Arguments:
- tokens: bfloat16 [3072, 1024], P(('dp', 'rows'), 'cols')
- lengths: int32 [2, 3], P('dp'), may hold values from 1 to 1534, as said below
- norm1_gain: float32 [1024], P('cols'), may hold values from 0.1 to 1.9
- w_in: bfloat16 [1024, 3, 1024], P('cols', None, 'rows'), may hold values from -0.1875 to 0.1875
- kernel: float32 [3, 1024], P(None, 'rows'), may hold values from -3.5 to 3.5
- w_out: bfloat16 [1024, 1024], P('rows', 'cols'), may hold values from -0.1875 to 0.1875
- norm2_gain: float32 [1024], P('cols'), may hold values from 0.1 to 1.9
- w_gate_up: bfloat16 [1024, 2, 4608], P('cols', None, 'rows'), may hold values from -0.1875 to 0.1875
- w_down: bfloat16 [4608, 1024], P('rows', 'cols'), may hold values from -0.09375 to 0.09375
- cotangent: bfloat16 [3072, 1024], P(('dp', 'rows'), 'cols'), may hold values from -6 to 6
Outputs:
- block_output: bfloat16 [3072, 1024], P(('dp', 'rows'), 'cols')
- input_grad: float32 [3072, 1024], P(('dp', 'rows'), 'cols')
- norm1_grad: float32 [1024], P('cols')
- w_in_grad: float32 [1024, 3, 1024], P('cols', None, 'rows')
- kernel_grad: float32 [3, 1024], P(None, 'rows')
- w_out_grad: float32 [1024, 1024], P('rows', 'cols')
- norm2_grad: float32 [1024], P('cols')
- w_gate_up_grad: float32 [1024, 2, 4608], P('cols', None, 'rows')
- w_down_grad: float32 [4608, 1024], P('rows', 'cols')
The draws below stay inside these ranges and needn't reach their ends.
Inputs may be any that keep to these rules, and one draw needn't show every extreme that they name: Each replica's lengths sum to at most 1536; its slots after them belong to no sequence.
All inputs are finite; a program needn't handle non-finite values.
Results may differ from the reference program's by a relative error of at most 0.0094.
Values may be sent and summed in bfloat16 or wider, within the bound.
No kernel may reach another device: no remote copies, remote signals or barrier semaphores. Data moves between devices by JAX's collectives and lax.ppermute only.
A program may use at most 128 MiB of HBM per device.

```python
import math
import jax
import jax.numpy as jnp
from jax import lax

D = 1024
FF = 4608
NSEQ = 3
TOK_REP = 1536
TOKENS = 3072
N_DP = 2


def draw_tokens(key, part):
    key = jax.random.fold_in(key, 5)
    key_base, key_rows, key_cols = jax.random.split(key, 3)
    rising = jnp.exp(math.log(3.0) * (jnp.arange(D, dtype=jnp.float32) / (D - 1) - 0.5))
    col_scale = rising * jnp.exp(jax.random.uniform(key_cols, (D,), minval=math.log(0.55), maxval=math.log(1.8)))
    row_scale = jnp.exp(jax.random.uniform(key_rows, (TOKENS, 1), minval=math.log(0.3), maxval=math.log(3.0)))
    base_values = jnp.clip(jax.random.normal(key_base, (TOKENS, D)), -4.0, 4.0)
    return (base_values * row_scale * col_scale[None, :]).astype(jnp.bfloat16)


def draw_lengths(key, part):
    key = jax.random.fold_in(key, 11)
    key_short, key_spare, key_long, key_pick = jax.random.split(key, 4)
    short_most = max(TOK_REP // 32, 2)
    short_lengths = jax.random.randint(key_short, (N_DP, NSEQ), 1, short_most + 1)
    spare_slots = jax.random.randint(key_spare, (N_DP, 1), 0, short_most)
    picked = jax.random.randint(key_pick, (), 0, N_DP)
    forced = (jnp.arange(N_DP, dtype=jnp.int32) == picked)[:, None]
    short_lengths = jnp.where(forced, 1, short_lengths)
    spare_slots = jnp.where(forced, 0, spare_slots)
    long_slot = jax.random.randint(key_long, (N_DP, 1), 0, NSEQ)
    slot_index = jnp.arange(NSEQ, dtype=jnp.int32)[None, :]
    is_long = slot_index == long_slot
    short_lengths = jnp.where(is_long, 0, short_lengths)
    long_length = TOK_REP - jnp.sum(short_lengths, axis=1, keepdims=True) - spare_slots
    return jnp.where(is_long, long_length, short_lengths).astype(jnp.int32)


def block_levels(stream_key, shape, pieces, low, top_value):
    def one(dim, parts):
        steps = jax.random.uniform(jax.random.fold_in(jax.random.fold_in(stream_key, 6), dim), (parts,), jnp.float32, low / len(pieces), top_value / len(pieces))
        return jnp.repeat(jnp.exp(steps), shape[dim] // parts).reshape((-1,) + (1,) * (len(shape) - dim - 1))

    loudness = one(*pieces[0])
    for cut in pieces[1:]:
        loudness = loudness * one(*cut)
    return loudness


def gaussian(own_key, shape, scale, reach, pieces=(), kind=jnp.bfloat16):
    array = jax.random.normal(own_key, shape, jnp.float32) * scale
    if len(pieces) > 0:
        array = block_levels(own_key, shape, pieces, -0.22, 0.18) * array
    return jnp.clip(array, min=-reach, max=reach).astype(kind)


def setup_inputs(seed: int = 0) -> dict:
    keys = jax.random.split(jax.random.key(seed), 11)
    tokens = draw_tokens(jax.random.fold_in(keys[10], 71), 0)
    lengths = draw_lengths(jax.random.fold_in(keys[10], 71), 0)
    norm1_gain = jnp.clip(1.0 + 0.18 * jax.random.normal(keys[2], (D,), jnp.float32), 0.1, 1.9)
    w_in = gaussian(keys[3], (D, 3, D), D ** -0.5, 0.1875, ((0, 4), (2, 4)))
    kernel = gaussian(keys[4], (3, D), 3 ** -0.5, 3.5, ((1, 4),), jnp.float32)
    w_out = gaussian(keys[5], (D, D), D ** -0.5, 0.1875, ((0, 4), (1, 4)))
    norm2_gain = jnp.clip(1.0 + 0.18 * jax.random.normal(keys[6], (D,), jnp.float32), 0.1, 1.9)
    w_gate_up = gaussian(keys[7], (D, 2, FF), D ** -0.5, 0.1875, ((0, 4), (2, 4)))
    w_down = gaussian(keys[8], (FF, D), FF ** -0.5, 0.09375, ((0, 4), (1, 4)))
    cotangent = gaussian(keys[9], (TOKENS, D), 1.0, 6.0, ((0, 8), (1, 4)))
    return {"tokens": tokens, "lengths": lengths, "norm1_gain": norm1_gain, "w_in": w_in, "kernel": kernel, "w_out": w_out, "norm2_gain": norm2_gain, "w_gate_up": w_gate_up, "w_down": w_down, "cotangent": cotangent}


EPS = 1e-06

@jax.custom_vjp
def low(v):
    return lax.optimization_barrier(v.astype(jnp.bfloat16)).astype(jnp.float32)

@jax.custom_vjp
def low_back(v):
    return v

def low_keep(v):
    return (low(v), None)

def low_pass(kept, grad):
    return (grad,)

def back_keep(v):
    return (v, None)

def back_low(kept, grad):
    return (low(grad),)
low.defvjp(low_keep, low_pass)
low_back.defvjp(back_keep, back_low)

def token_taps(seq_lengths, first_token, token_count):
    seq_ends = jnp.cumsum(seq_lengths).astype(jnp.int32)
    position = (first_token + jnp.arange(token_count, dtype=jnp.int32)).astype(jnp.int32)
    finished = seq_ends[None, :] <= position[:, None]
    seq_start = lax.optimization_barrier(jnp.sum(jnp.where(finished, seq_lengths[None, :], 0), axis=1)).astype(jnp.int32)
    offset = position - seq_start
    living = position < seq_ends[-1]
    tap_list = [jnp.logical_and(living, offset >= lag_step) for lag_step in range(3)]
    return jnp.stack(tap_list, axis=1).astype(jnp.float32)

def matmul(left_side, right_side):
    return jnp.dot(left_side, right_side, precision=lax.Precision.HIGHEST)

def rms_scale(values, gain):
    inverse = lax.rsqrt(lax.optimization_barrier(jnp.mean(values * values, axis=1, keepdims=True)) + EPS)
    return values * inverse * gain

def replica_forward(resid_in, tap_masks, params):
    gain_one, w_in, kernel, w_out, gain_two, w_gate_up, w_down = params
    rows_here = resid_in.shape[0]
    normed_one = low(rms_scale(resid_in, gain_one))
    projected = low_back(matmul(normed_one, w_in.reshape(D, 3 * D))).reshape(rows_here, 3, D)
    b_part, c_part, v_part = (projected[:, 0], projected[:, 1], projected[:, 2])
    product_bv = low(b_part * v_part)
    padded = jnp.concatenate([jnp.zeros((2, D), jnp.float32), product_bv], axis=0)
    conv_out = jnp.zeros((rows_here, D), jnp.float32)
    for lag_step in range(3):
        conv_out = conv_out + kernel[lag_step] * tap_masks[:, lag_step:lag_step + 1] * padded[2 - lag_step:2 - lag_step + rows_here]
    conv_out = low_back(conv_out)
    mixed_in = low(c_part * conv_out)
    resid_mid = resid_in + low_back(matmul(mixed_in, w_out))
    normed_two = low(rms_scale(resid_mid, gain_two))
    gate_up = low_back(matmul(normed_two, w_gate_up.reshape(D, 2 * FF)))
    activated = low(jax.nn.silu(gate_up[:, :FF]) * gate_up[:, FF:])
    return resid_mid + matmul(activated, w_down)

def reference(tokens, lengths, norm1_gain, w_in, kernel, w_out, norm2_gain, w_gate_up, w_down, cotangent):
    params = (norm1_gain, w_in.astype(jnp.float32), kernel, w_out.astype(jnp.float32), norm2_gain, w_gate_up.astype(jnp.float32), w_down.astype(jnp.float32))
    inputs = tokens.astype(jnp.float32).reshape(N_DP, TOK_REP, D)
    grads_in = cotangent.astype(jnp.float32).reshape(N_DP, TOK_REP, D)

    def replica_step(totals, slices):
        resid_in, grad_out, seq_lengths = slices
        tap_masks = token_taps(seq_lengths, 0, TOK_REP)

        def forward(values, weights):
            return replica_forward(values, tap_masks, weights)
        result, pullback = jax.vjp(forward, resid_in, params)
        grad_input, grad_params = pullback(grad_out)
        totals = jax.tree.map(lambda first_tree, second_tree: first_tree + second_tree, totals, grad_params)
        return (totals, (result, grad_input))
    zero_grads = jax.tree.map(jnp.zeros_like, params)
    totals, (results, grad_rows) = lax.scan(replica_step, zero_grads, (inputs, grads_in, lengths))
    return (results.reshape(TOKENS, D).astype(jnp.bfloat16), grad_rows.reshape(TOKENS, D), totals[0], totals[1], totals[2], totals[3], totals[4], totals[5], totals[6])
```

```python
import jax
import jax.numpy as jnp
from jax import lax
from jax.sharding import PartitionSpec as P

EPS = 1e-06
BF = jnp.bfloat16
F32 = jnp.float32


def swap(value, axis, bit):
    size = lax.axis_size(axis)
    return lax.ppermute(value, axis, [(i, i ^ bit) for i in range(size)])


def dot(a, b, dims=((1,), (0,))):
    return lax.dot_general(a, b, (dims, ((), ())), preferred_element_type=F32)


def rounded(v):
    return lax.reduce_precision(v, 8, 7).astype(BF)


def bits_of(size):
    bits = []
    bit = 1
    while bit < size:
        bits.append(bit)
        bit *= 2
    return bits


def spread(value, axis):
    held = {0: value}
    for bit in reversed(bits_of(lax.axis_size(axis))):
        for k in list(held):
            held[k ^ bit] = swap(held[k], axis, bit)
    return [held[k] for k in range(len(held))]


def direct(blocks, axis):
    return [blocks[0]] + [swap(blocks[k], axis, k) for k in range(1, len(blocks))]


def fold(blocks, axis, low):
    left = list(blocks)
    for bit in bits_of(len(left)):
        left_k = [k for k in range(len(left)) if left[k] is not None]
        for k in left_k:
            if k & bit:
                continue
            sent = left[k | bit]
            sent = rounded(sent) if low else sent
            left[k] = left[k] + swap(sent, axis, bit).astype(F32)
        for k in left_k:
            if k & bit:
                left[k] = None
    return left[0]


def total_dp(value):
    if lax.axis_size("dp") == 2:
        mine = rounded(value)
        return mine.astype(F32) + swap(mine, "dp", 1).astype(F32)
    return lax.psum(value, "dp")


def butterfly(value, axis):
    for bit in bits_of(lax.axis_size(axis)):
        value = value + swap(value, axis, bit)
    return value


def taps_at(seq_lengths, position):
    seq_ends = jnp.cumsum(seq_lengths)
    finished = seq_ends <= position[..., None]
    seq_start = jnp.sum(jnp.where(finished, seq_lengths, 0), axis=-1)
    offset = position - seq_start
    living = position < seq_ends[-1]
    return [jnp.logical_and(living, offset >= lag).astype(F32)[..., None] for lag in range(3)]


def pick(blocks, index):
    rows = []
    for j in range(len(blocks)):
        row = jnp.zeros_like(blocks[0])
        for i in range(len(blocks)):
            row = jnp.where(index[j] == i, blocks[i], row)
        rows.append(row)
    return jnp.stack(rows)


def local(tokens, lengths, gain1, w_in, kernel, w_out, gain2, w_gu, w_down, cotangent):
    shard, feats = tokens.shape
    R, C = lax.axis_size("rows"), lax.axis_size("cols")
    z, c = lax.axis_index("rows"), lax.axis_index("cols")
    Q = shard // C
    T = R * Q
    D = C * feats
    width = w_out.shape[0]
    hidden = w_down.shape[0]

    def to_tokens(a):
        parts = [lax.dynamic_slice_in_dim(a, (c ^ k) * Q, Q, 0) for k in range(C)]
        return jnp.concatenate(direct(parts, "cols"), axis=1)

    def to_shard(a):
        parts = direct([a[:, k * feats : (k + 1) * feats] for k in range(C)], "cols")
        out = jnp.zeros((shard, feats), a.dtype)
        for k in range(C):
            out = lax.dynamic_update_slice_in_dim(out, parts[k], (c ^ k) * Q, 0)
        return out

    def gather_rows(a):
        return jnp.concatenate(direct([a] * R, "rows"), axis=0)

    def scatter_rows(partial):
        parts = [partial[k * Q : (k + 1) * Q] for k in range(R)]
        got = direct([parts[0]] + [rounded(p) for p in parts[1:]], "rows")
        out = got[0]
        for g in got[1:]:
            out = out + g.astype(F32)
        return out

    x_own = to_tokens(tokens)
    x_all = gather_rows(x_own)
    gains = [jnp.concatenate(g) for g in zip(*[(g[0], g[1]) for g in spread(jnp.stack([gain1, gain2]), "cols")])]
    g1, g2 = gains
    w_in_flat = w_in.reshape(feats, 3 * width)
    w_in_all = jnp.concatenate(spread(w_in_flat, "cols"), axis=0)
    w_out_tall = jnp.concatenate(direct([w_out] * R, "rows"), axis=0)
    w_out_all = jnp.concatenate(spread(w_out_tall, "cols"), axis=1)
    dy_own = to_tokens(cotangent)
    dy_all = gather_rows(dy_own)
    w_gu_all = jnp.concatenate(spread(w_gu.reshape(feats, 2 * hidden), "cols"), axis=0)
    w_down_all = jnp.concatenate(spread(w_down, "cols"), axis=1)

    position = jnp.stack([(z ^ j) * shard + c * Q + jnp.arange(Q, dtype=jnp.int32) for j in range(R)])
    taps = taps_at(lengths[0], position)
    taps_next = taps_at(lengths[0], position + 1), taps_at(lengths[0], position + 2)

    x = x_all.astype(F32)
    inv1 = lax.rsqrt(jnp.mean(x * x, axis=1, keepdims=True) + EPS)
    normed1 = (x * inv1 * g1).astype(BF)
    proj = dot(normed1, w_in_all).reshape(R, Q, 3 * width)
    b_part, c_part, v_part = (proj[..., i * width : (i + 1) * width] for i in range(3))
    bv = (b_part * v_part).astype(BF)
    ring = [(i, (i + 1) % C) for i in range(C)]
    before = lax.ppermute(bv[:, Q - 2 :], "cols", ring)
    first, last = c == 0, c == C - 1
    before = pick(
        [before[j] for j in range(R)],
        [jnp.where(first, jnp.where((z ^ j) == 0, -1, ((z ^ j) - 1) ^ z), j) for j in range(R)],
    )
    wide = jnp.concatenate([before, bv], axis=1).astype(F32)
    lagged = [wide[:, 2 - lag : 2 - lag + Q] for lag in range(3)]
    conv = kernel[0] * taps[0] * lagged[0] + kernel[1] * taps[1] * lagged[1] + kernel[2] * taps[2] * lagged[2]
    mixin = (c_part * conv).astype(BF)
    mix_parts = direct([jnp.stack([mixin[j ^ k] for j in range(R)]) for k in range(R)], "rows")
    mix_all = jnp.concatenate([m.reshape(T, width) for m in mix_parts], axis=1)
    mid = x + dot(mix_all, w_out_all)

    inv2 = lax.rsqrt(jnp.mean(mid * mid, axis=1, keepdims=True) + EPS)
    normed2 = (mid * inv2 * g2).astype(BF)
    gu = dot(normed2, w_gu_all)
    gate, up = gu[:, :hidden], gu[:, hidden:]
    sig = jax.nn.sigmoid(gate)
    act = (gate * sig * up).astype(BF)
    out_own = mid[:Q] + scatter_rows(dot(act, w_down_all))
    block_output = to_shard(out_own.astype(BF))

    grad_act = dot(dy_all, w_down_all, ((1,), (1,)))
    grad_gate = grad_act * up * sig * (1.0 + gate * (1.0 - sig))
    grad_up = grad_act * gate * sig
    grad_gu = jnp.concatenate([grad_gate, grad_up], axis=1).astype(BF)
    gn2 = dot(grad_gu, w_gu_all, ((1,), (1,)))
    norm2_part = jnp.sum(gn2 * mid * inv2, axis=0)
    gn2_own = scatter_rows(gn2)
    mid_own, inv2_own = mid[:Q], inv2[:Q]
    scaled = gn2_own * g2
    inner = jnp.mean(scaled * mid_own, axis=1, keepdims=True)
    grad_mid = dy_own.astype(F32) + inv2_own * scaled - mid_own * (inv2_own**3 * inner)
    gm_all = gather_rows(grad_mid.astype(BF))

    def over_cols(g, dim):
        return total_dp(fold(jnp.split(g, C, axis=dim), "cols", True))

    down_grad = over_cols(dot(act, dy_all, ((0,), (0,))), 1)
    gu_grad = over_cols(dot(normed2, grad_gu, ((0,), (0,))), 0).reshape(feats, 2, hidden)

    mixin_flat = mixin.reshape(T, width)
    out_grad = over_cols(dot(mixin_flat, gm_all, ((0,), (0,))), 1)
    grad_mix = dot(gm_all, w_out_all[:width], ((1,), (1,))).reshape(R, Q, width)
    grad_c = grad_mix * conv
    grad_conv = (grad_mix * c_part).astype(BF)
    back = [(i, (i - 1) % C) for i in range(C)]
    after = lax.ppermute(grad_conv[:, :2], "cols", back)
    after = pick(
        [after[j] for j in range(R)],
        [jnp.where(last, jnp.where((z ^ j) == R - 1, -1, ((z ^ j) + 1) ^ z), j) for j in range(R)],
    )
    gwide = jnp.concatenate([grad_conv, after], axis=1).astype(F32)
    grad_conv_f = grad_conv.astype(F32)
    grad_bv = (
        kernel[0] * taps[0] * grad_conv_f
        + kernel[1] * taps_next[0][1] * gwide[:, 1 : 1 + Q]
        + kernel[2] * taps_next[1][2] * gwide[:, 2 : 2 + Q]
    )
    kernel_part = jnp.stack([jnp.sum(grad_conv_f * taps[lag] * lagged[lag], axis=(0, 1)) for lag in range(3)])
    grad_proj = jnp.concatenate([grad_bv * v_part, grad_c, grad_bv * b_part], axis=2).astype(BF).reshape(T, 3 * width)
    gn1 = dot(grad_proj, w_in_all, ((1,), (1,)))
    norm1_part = jnp.sum(gn1 * x * inv1, axis=0)
    gn1_own = scatter_rows(gn1)
    in_grad = over_cols(dot(normed1, grad_proj, ((0,), (0,))), 0).reshape(feats, 3, width)
    x_own_f, inv1_own = x[:Q], inv1[:Q]
    scaled1 = gn1_own * g1
    inner1 = jnp.mean(scaled1 * x_own_f, axis=1, keepdims=True)
    input_own = grad_mid + inv1_own * scaled1 - x_own_f * (inv1_own**3 * inner1)
    input_grad = to_shard(input_own)

    kernel_grad = butterfly(kernel_part, "cols")
    norms = jnp.stack([norm1_part.reshape(C, feats), norm2_part.reshape(C, feats)], axis=1)
    norms = fold([norms[k] for k in range(C)], "cols", False)
    small = jnp.concatenate([kernel_grad, norms], axis=0)
    small = butterfly(small, "dp")
    kernel_grad = small[:3]
    norms = butterfly(small[3:], "rows")
    return (
        block_output,
        input_grad,
        norms[0],
        in_grad,
        kernel_grad,
        out_grad,
        norms[1],
        gu_grad,
        down_grad,
    )


def solution(mesh):
    tok = P(("dp", "rows"), "cols")
    feat = P("cols")
    wide = P("cols", None, "rows")
    tall = P("rows", "cols")
    taps = P(None, "rows")
    return jax.shard_map(
        local,
        mesh=mesh,
        in_specs=(tok, P("dp", None), feat, wide, taps, tall, feat, wide, tall, tok),
        out_specs=(tok, tok, feat, wide, taps, tall, feat, wide, tall),
        check_vma=False,
    )
```

```python
import functools

import jax
import jax.numpy as jnp
from jax import lax
from jax.experimental import pallas as pl
from jax.experimental.pallas import tpu as pltpu
from jax.sharding import PartitionSpec as P

EPS = 1e-06
BF = jnp.bfloat16
F32 = jnp.float32
EDGE = 8


def swap(value, axis, bit):
    size = lax.axis_size(axis)
    return lax.ppermute(value, axis, [(i, i ^ bit) for i in range(size)])


def dot(a, b):
    return jnp.dot(a, b, preferred_element_type=F32)


def dot_t(a, b):
    return lax.dot_general(a, b, (((1,), (1,)), ((), ())), preferred_element_type=F32)


def t_dot(a, b):
    return lax.dot_general(a, b, (((0,), (0,)), ((), ())), preferred_element_type=F32)


def low(v):
    return lax.reduce_precision(v, 8, 7).astype(BF)


def after(value, *first):
    return lax.optimization_barrier((value,) + first)[0]


def pick(blocks, index):
    rows = []
    for wanted in index:
        row = jnp.zeros_like(blocks[0])
        for i, block in enumerate(blocks):
            row = jnp.where(wanted == i, block, row)
        rows.append(row)
    return rows


def cat(parts, dim):
    return jnp.concatenate(parts, axis=dim)


def on_core(body, out, scratch=(), flops=0):
    vmem = pl.BlockSpec(memory_space=pltpu.VMEM)
    smem = pl.BlockSpec(memory_space=pltpu.SMEM)

    def call(*args, scalars=0):
        return pl.pallas_call(
            body,
            out_shape=out,
            in_specs=[smem] * scalars + [vmem] * (len(args) - scalars),
            out_specs=[vmem] * len(out),
            scratch_shapes=list(scratch),
            compiler_params=pltpu.CompilerParams(vmem_limit_bytes=48 * 2**20),
            cost_estimate=pl.CostEstimate(flops=flops, bytes_accessed=sum(a.size * a.dtype.itemsize for a in args), transcendentals=0),
        )(*args)

    return call


def shape(dims, kind):
    return jax.ShapeDtypeStruct(dims, kind)


def place_body(tokens, cotangent, gain1, gain2, *outs):
    S = tokens.shape[0]
    Q = S // 4
    c = lax.axis_index("cols")
    rows = lax.broadcasted_iota(jnp.int32, (EDGE, tokens.shape[1]), 0)
    gains = jnp.zeros(rows.shape, F32)
    at = 0
    for gain in (gain1[...], gain2[...]):
        rest = gain
        for _ in range(3):
            part = rest.astype(BF).astype(F32)
            rest = rest - part
            gains = jnp.where(rows == at, part, gains)
            at += 1
    for k in range(4):
        start = pl.multiple_of((c ^ k) * Q, 16)
        early = pl.multiple_of(lax.rem(start + S - 16, S), 16)
        edge = tokens[pl.ds(early, 16), :].astype(F32)[EDGE:]
        outs[k][:Q, :] = tokens[pl.ds(start, Q), :]
        outs[k][Q:, :] = jnp.concatenate([edge, gains], axis=0).astype(BF)
        outs[4 + k][...] = cotangent[pl.ds(start, Q), :]


def join_body(twin, p0, p2, p1, p3, x_ref, g_ref):
    y = lax.axis_index("dp")
    rows = x_ref.shape[0]
    F = p0.shape[1]
    half = F // 2
    for i, piece in enumerate((p0, p2, p1, p3)):
        v = piece[...].astype(F32)
        if i % 2 and twin:
            turned = jnp.concatenate([v[:, half:], v[:, :half]], axis=1)
            v = jnp.where(y == 0, v, turned)
        x_ref[:, i * F : (i + 1) * F] = v[:rows].astype(BF)
        t = v[rows:]
        g_ref[0:1, i * F : (i + 1) * F] = (t[0:1] + t[1:2]) + t[2:3]
        g_ref[1:2, i * F : (i + 1) * F] = (t[3:4] + t[4:5]) + t[5:6]


def chunk_taps(lengths, j, S, Q, W):
    z, c = lax.axis_index("rows"), lax.axis_index("cols")
    place = (z ^ j) * S + c * Q + lax.broadcasted_iota(jnp.int32, (Q, W), 0)
    end = jnp.int32(0)
    start = jnp.zeros_like(place)
    for i in range(lengths.shape[1]):
        end = end + lengths[0, i]
        start = jnp.where(place >= end, end, start)
    return [jnp.logical_and(place < end, place - start >= lag) for lag in range(3)]


def neighbour(j):
    z, c = lax.axis_index("rows"), lax.axis_index("cols")
    return jnp.where(c == 0, lax.rem((z ^ j) + 3, 4) ^ z, j)


def edge_products(proj_ref, edges, T, W):
    for j in range(4):
        lo = T + j * EDGE
        edges[j] = (proj_ref[lo : lo + EDGE, :W] * proj_ref[lo : lo + EDGE, 2 * W :]).astype(BF).astype(F32)


def tapped_lags(proj_ref, edges, taps, j, Q, W):
    lo = j * Q
    bv = (proj_ref[lo : lo + Q, :W] * proj_ref[lo : lo + Q, 2 * W :]).astype(BF).astype(F32)
    edge = edges[neighbour(j)]
    row = lax.broadcasted_iota(jnp.int32, (Q, W), 0)
    one = jnp.where(row == 0, edge[EDGE - 1 :], pltpu.roll(bv, 1, 0))
    two = pltpu.roll(bv, 2, 0)
    two = jnp.where(row == 0, edge[EDGE - 2 : EDGE - 1], jnp.where(row == 1, edge[EDGE - 1 :], two))
    return [jnp.where(tap, lagged, 0.0) for tap, lagged in zip(taps, (bv, one, two))]


def fill(scratch, pieces, dim):
    at = 0
    for piece in pieces:
        size = piece.shape[dim]
        if dim == 0:
            scratch[at : at + size, :] = piece[...]
        else:
            scratch[:, at : at + size] = piece[...]
        at += size


def split(refs, *counts):
    out = []
    for n in counts:
        out.append(refs[:n])
        refs = refs[n:]
    return out + [refs]


def mixer_body(np_, lengths, *refs):
    xs, (gain, kernel), ws, rest = split(refs, 4, 2, np_)
    normed, proj, mixin, edges, w = rest
    Q = xs[0].shape[0] - EDGE
    T = 4 * Q
    W = kernel.shape[1]
    fill(w, ws, 0)
    tail = []
    for j, part in enumerate(xs):
        v = part[...].astype(F32)
        inv = lax.rsqrt(jnp.mean(v * v, axis=1, keepdims=True) + EPS)
        n = v * inv * gain[0:1, :]
        normed[j * Q : (j + 1) * Q, :] = n[:Q].astype(BF)
        tail.append(n[Q:])
    normed[T:, :] = jnp.concatenate(tail, axis=0).astype(BF)
    for i in range(3):
        cols = slice(i * W, (i + 1) * W)
        proj[:, cols] = dot(normed[...], w[:, cols])
    edge_products(proj, edges, T, W)
    for j in range(4):
        taps = chunk_taps(lengths, j, 4 * Q, Q, W)
        lags = tapped_lags(proj, edges, taps, j, Q, W)
        conv = kernel[0:1, :] * lags[0] + kernel[1:2, :] * lags[1] + kernel[2:3, :] * lags[2]
        mixin[j * Q : (j + 1) * Q, :] = (proj[j * Q : (j + 1) * Q, W : 2 * W] * conv).astype(BF)


def hidden_tiles(H):
    return [(h, min(256, H - h)) for h in range(0, H, 256)]


def fill_out(scratch, pieces, twin):
    if not twin:
        return fill(scratch, pieces, 1)
    y = lax.axis_index("dp")
    n = pieces[0].shape[1]
    for h in range(2):
        a, b, c, d = pieces[4 * h : 4 * h + 4]
        at = 4 * n * h
        first, second = a[...].astype(F32), b[...].astype(F32)
        scratch[:, at : at + n] = jnp.where(y == 0, first, second).astype(BF)
        scratch[:, at + n : at + 2 * n] = jnp.where(y == 0, second, first).astype(BF)
        scratch[:, at + 2 * n : at + 3 * n] = c[...]
        scratch[:, at + 3 * n : at + 4 * n] = d[...]


def forward_body(no, ng, twin, *refs):
    xs, ms, (gain,), wos, wgs, rest = split(refs, 4, 4, 1, no, ng)
    mid_own, normed, xhat, act, slope, silu_ref, mid, wo, wg = rest
    T = ms[0].shape[0]
    Q = T // 4
    H = act.shape[1]
    gain2 = gain[1:2, :]
    fill_out(wo, wos, twin)
    fill(wg, wgs, 0)
    for j in range(4):
        rows = slice(j * Q, (j + 1) * Q)
        mix = jnp.concatenate([ms[k][(j ^ k) * Q : ((j ^ k) + 1) * Q, :] for k in range(4)], axis=1)
        mid[rows, :] = xs[j][:Q, :].astype(F32) + dot(mix, wo[...])
        v = mid[rows, :]
        inv = lax.rsqrt(jnp.mean(v * v, axis=1, keepdims=True) + EPS)
        xhat[rows, :] = v * inv
        normed[rows, :] = (v * inv * gain2).astype(BF)
    mid_own[...] = mid[:Q, :]
    for h, size in hidden_tiles(H):
        cols, ups = slice(h, h + size), slice(H + h, H + h + size)
        gate = dot(normed[...], wg[:, cols])
        up = dot(normed[...], wg[:, ups])
        sig = 1.0 / (1.0 + jnp.exp(-gate))
        silu = gate * sig
        act[:, cols] = (silu * up).astype(BF)
        silu_ref[:, cols] = silu
        slope[:, cols] = up * sig * (1.0 + gate * (1.0 - sig))


def turn_body(nd, *refs):
    ds, wds, (slope, silu, act, normed), rest = split(refs, 4, nd, 4)
    gg, gu, dy_all, sent_down, sent_gate, sent_up, wd = rest
    Q = ds[0].shape[0]
    H = act.shape[1]
    DH = normed.shape[1] // 2
    fill(wd, wds, 1)
    for j, d in enumerate(ds):
        dy_all[j * Q : (j + 1) * Q, :] = d[...]
    for h, size in hidden_tiles(H):
        cols = slice(h, h + size)
        grad = dot_t(dy_all[...], wd[cols, :])
        gu[:, cols] = (grad * silu[:, cols]).astype(BF)
        gg[:, cols] = (grad * slope[:, cols]).astype(BF)
    for h, size in hidden_tiles(H):
        cols = slice(h, h + size)
        sent_down[cols, :] = t_dot(act[:, cols], dy_all[:, DH:]).astype(BF)
        sent_gate[:, cols] = t_dot(normed[:, DH:], gg[:, cols]).astype(BF)
        sent_up[:, cols] = t_dot(normed[:, DH:], gu[:, cols]).astype(BF)


def through_body(ng, *refs):
    wgs, (gg, gu, xhat), rest = split(refs, ng, 3)
    own, s1, s2, s3, norm_part, wg = rest
    Q = own.shape[0]
    D = own.shape[1]
    H = gg.shape[1]
    fill(wg, wgs, 0)
    for n in range(0, D, 256):
        cols = slice(n, n + 256)
        v = dot_t(gg[...], wg[cols, :H]) + dot_t(gu[...], wg[cols, H:])
        norm_part[0:1, cols] = jnp.sum(v * xhat[:, cols], axis=0, keepdims=True)
        own[:, cols] = v[:Q]
        for k, out in ((1, s1), (2, s2), (3, s3)):
            out[:, cols] = v[k * Q : (k + 1) * Q].astype(BF)


def flipped_halves(v, dim, twin):
    if not twin:
        return v
    y = lax.axis_index("dp")
    n = v.shape[dim] // 2
    a, b = (v[:n], v[n:]) if dim == 0 else (v[:, :n], v[:, n:])
    return jnp.concatenate([jnp.where(y == 0, a, b), jnp.where(y == 0, b, a)], axis=dim)


def keep_rows_body(twin, left, right, got, mine, theirs):
    F = mine.shape[0]
    for h, size in hidden_tiles(right.shape[1]):
        cols = slice(h, h + size)
        v = t_dot(left[:, : 2 * F], right[:, cols]) + got[:, cols].astype(F32)
        mine[:, cols] = v[:F]
        theirs[:, cols] = flipped_halves(v[F:], 0, twin).astype(BF)


def keep_cols_body(twin, left, right, got, mine, theirs):
    F = mine.shape[1]
    for h, size in hidden_tiles(left.shape[1]):
        rows = slice(h, h + size)
        v = t_dot(left[:, rows], right[:, : 2 * F]) + got[rows, :].astype(F32)
        mine[rows, :] = v[:, :F]
        theirs[rows, :] = flipped_halves(v[:, F:], 1, twin).astype(BF)


def back_body(no, twin, lengths, *refs):
    gs, wos, xs, (kernel, proj, mixin, normed), rest = split(refs, 4, no, 4, 4)
    gproj, gm_all, xhat, sent_out, sent_in, kernel_part, edges, back, wo = rest
    Q = gs[0].shape[0]
    T = 4 * Q
    W = kernel.shape[1]
    DH = wo.shape[1] // 2
    row = lax.broadcasted_iota(jnp.int32, (Q, W), 0)
    fill_out(wo, wos, twin)
    edge_products(proj, edges, T, W)
    back[...] = jnp.zeros(back.shape, F32)
    sums = [jnp.zeros((1, W), F32)] * 3
    tail = []
    for j, (part, xp) in enumerate(zip(gs, xs)):
        rows = slice(j * Q, (j + 1) * Q)
        gm_all[rows, :] = part[...]
        v = xp[...].astype(F32)
        v = v * lax.rsqrt(jnp.mean(v * v, axis=1, keepdims=True) + EPS)
        xhat[rows, :] = v[:Q]
        xhat[T + j * EDGE : T + (j + 1) * EDGE, :] = v[Q:]
        grad_mix = dot_t(part[...], wo[...])
        taps = chunk_taps(lengths, j, 4 * Q, Q, W)
        lags = tapped_lags(proj, edges, taps, j, Q, W)
        conv = kernel[0:1, :] * lags[0] + kernel[1:2, :] * lags[1] + kernel[2:3, :] * lags[2]
        grad_conv = (grad_mix * proj[rows, W : 2 * W]).astype(BF).astype(F32)
        sums = [s + jnp.sum(grad_conv * lag, axis=0, keepdims=True) for s, lag in zip(sums, lags)]
        m0, m1, m2 = [jnp.where(tap, grad_conv, 0.0) for tap in taps]
        m1 = kernel[1:2, :] * m1
        m2 = kernel[2:3, :] * m2
        grad_bv = kernel[0:1, :] * m0
        grad_bv = grad_bv + jnp.where(row < Q - 1, pltpu.roll(m1, Q - 1, 0), 0.0)
        grad_bv = grad_bv + jnp.where(row < Q - 2, pltpu.roll(m2, Q - 2, 0), 0.0)
        head = lax.broadcasted_iota(jnp.int32, (EDGE, W), 0)
        last = jnp.where(head == EDGE - 1, m1[0:1] + m2[1:2], 0.0)
        back[neighbour(j)] = jnp.where(head == EDGE - 2, m2[0:1], last)
        gproj[rows, :W] = (grad_bv * proj[rows, 2 * W :]).astype(BF)
        gproj[rows, W : 2 * W] = (grad_mix * conv).astype(BF)
        gproj[rows, 2 * W :] = (grad_bv * proj[rows, :W]).astype(BF)
    for i in range(3):
        kernel_part[i : i + 1, :] = sums[i]
    for j in range(4):
        lo = T + j * EDGE
        tail.append(
            jnp.concatenate(
                [back[j] * proj[lo : lo + EDGE, 2 * W :], jnp.zeros((EDGE, W), F32), back[j] * proj[lo : lo + EDGE, :W]],
                axis=1,
            )
        )
    gproj[T:, :] = jnp.concatenate(tail, axis=0).astype(BF)
    sent_out[...] = t_dot(mixin[...], gm_all[:, DH:]).astype(BF)
    for i in range(3):
        cols = slice(i * W, (i + 1) * W)
        sent_in[:, cols] = t_dot(normed[:, DH:], gproj[:, cols]).astype(BF)


def last_body(ni, *refs):
    ws, (gproj, xhat), rest = split(refs, ni, 2)
    own, s1, s2, s3, norm_part, w = rest
    E, D = own.shape
    Q = E - EDGE
    T = 4 * Q
    fill(w, ws, 0)
    for n in range(0, D, 256):
        cols = slice(n, n + 256)
        v = dot_t(gproj[...], w[cols, :])
        norm_part[0:1, cols] = jnp.sum(v * xhat[:, cols], axis=0, keepdims=True)
        for k, out in enumerate((own, s1, s2, s3)):
            part = jnp.concatenate([v[k * Q : (k + 1) * Q], v[T + k * EDGE : T + (k + 1) * EDGE]], axis=0)
            out[:, cols] = part.astype(out.dtype)


def local(tokens, lengths, gain1, w_in, kernel, w_out, gain2, w_gu, w_down, cotangent):
    S, F = tokens.shape
    R, C = lax.axis_size("rows"), lax.axis_size("cols")
    assert R == 4 and C == 4
    z, c, y = lax.axis_index("rows"), lax.axis_index("cols"), lax.axis_index("dp")
    twin = lax.axis_size("dp") == 2
    Q = S // C
    E = Q + EDGE
    T = R * Q
    TE = R * E
    W = w_out.shape[0]
    H = w_down.shape[0]
    D = C * F
    DH = 2 * F
    half = F // 2

    def flip(v, dim):
        if not twin:
            return v
        a, b = jnp.split(v, 2, axis=dim)
        return cat([jnp.where(y == 0, a, b), jnp.where(y == 0, b, a)], dim)

    def half_y(v, dim):
        a, b = jnp.split(v, 2, axis=dim)
        return jnp.where(y == 0, a, b)

    def far(v, dim):
        if not twin:
            return [swap(v, "cols", 2)]
        first = swap(half_y(v, dim), "cols", 2)
        return [first, swap(first, "dp", 1)]

    order = (0, 2, 1, 3)

    def exchange(pieces):
        return [pieces[0]] + [swap(pieces[k], "cols", k) for k in (1, 2, 3)]

    def gather_rows(a):
        far_two = swap(a, "rows", 2)
        far_three = swap(a, "rows", 3)
        return [a, swap(a, "rows", 1), far_two, far_three]

    def scatter_rows(own, sent):
        got = [swap(sent[k - 1], "rows", k) for k in (2, 3, 1)]
        for g in got:
            own = own + g.astype(F32)
        return own

    def cross(v):
        return lax.ppermute(v, ("dp", "cols"), [(p * C + i, (1 - p) * C + (i ^ 1)) for p in range(2) for i in range(C)])

    def hop(v, dim):
        return swap(half_y(v, dim) if twin else v, "cols", 2)

    def over(v):
        return swap(v, "dp", 1)

    def near(*vs):
        return [swap(v, "cols", 1) for v in vs]

    join = lax.optimization_barrier
    weights = [w_in.reshape(F, 3 * W), w_out, w_gu.reshape(F, 2 * H), w_down]

    placed = on_core(place_body, [shape((E + EDGE, F), BF)] * 4 + [shape((Q, F), BF)] * 4)(
        tokens, cotangent, gain1.reshape(1, F), gain2.reshape(1, F)
    )
    wi, wo, wg, wd = weights
    wo = half_y(wo, 1) if twin else wo
    pieces, wi_far, wo_parts = join((exchange(placed[:4]), hop(wi, 0), gather_rows(wo)))
    x_own, gains = on_core(functools.partial(join_body, twin), [shape((E, D), BF), shape((2, D), F32)])(
        *[pieces[k] for k in order]
    )

    wo = cat(wo_parts, 0)
    x_own, wo, wi, wi_far, wg, placed = join((x_own, wo, wi, wi_far, wg, placed))
    x_parts = gather_rows(x_own)
    if twin:
        wi_pieces = [wi, wi_far, over(wi_far)] + near(wi, wi_far) + [cross(wi_far)]
        wo_other = [over(wo)]
    else:
        wi_pieces = [wi, wi_far] + near(wi, wi_far)
        wo_other = []
    wo_far = swap(wo, "cols", 2)
    wg_far = hop(wg, 0)
    x_parts, wi_pieces, wo_other, wo_far, wg_far = join((x_parts, wi_pieces, wo_other, wo_far, wg_far))

    normed1, proj, mixin = on_core(
        functools.partial(mixer_body, len(wi_pieces)),
        [shape((TE, D), BF), shape((TE, 3 * W), F32), shape((T, W), BF)],
        [pltpu.VMEM((R, EDGE, W), F32), pltpu.VMEM((D, 3 * W), BF)],
    )(lengths, *x_parts, gains, kernel, *wi_pieces, scalars=1)

    mixin, wo, wo_other, wo_far, wg, wg_far, wd, dy_pieces = join(
        (mixin, wo, wo_other, wo_far, wg, wg_far, wd, placed[4:])
    )
    mix_parts = gather_rows(mixin)
    dy_pieces = exchange(dy_pieces)
    wd_far = hop(wd, 1)
    wo_near = near(wo, *wo_other, wo_far)
    wg_near = near(wg, wg_far)
    wo_rest = [over(wo_far)] if twin else []
    wg_rest = [over(wg_far)] if twin else []
    mix_parts, dy_pieces, wd_far, wo_near, wg_near, wo_rest, wg_rest, wd = join(
        (mix_parts, dy_pieces, wd_far, wo_near, wg_near, wo_rest, wg_rest, wd)
    )
    wo_pieces = [wo] + wo_other + [wo_far] + wo_rest + wo_near + near(*wo_rest)
    wg_pieces = [wg, wg_far] + wg_rest + wg_near + near(*wg_rest)
    dy_own = cat([dy_pieces[k] if k < 2 else flip(dy_pieces[k], 1) for k in order], 1)

    dy_own, wd, wd_far, wo_pieces, wg_pieces = join((dy_own, wd, wd_far, wo_pieces, wg_pieces))
    dy_parts = gather_rows(dy_own)
    if twin:
        wd_pieces = [wd, wd_far, over(wd_far)] + near(wd, wd_far) + [cross(wd_far)]
    else:
        wd_pieces = [wd, wd_far] + near(wd, wd_far)
    mid_own, normed2, xhat2, act, slope, silu = on_core(
        functools.partial(forward_body, len(wo_pieces), len(wg_pieces), twin),
        [shape((Q, D), F32), shape((T, D), BF), shape((T, D), F32), shape((T, H), BF), shape((T, H), F32), shape((T, H), F32)],
        [pltpu.VMEM((T, D), F32), pltpu.VMEM((D, D), BF), pltpu.VMEM((D, 2 * H), BF)],
    )(*x_parts, *mix_parts, gains, *wo_pieces, *wg_pieces)
    dy_parts, wd_pieces, act = join((dy_parts, wd_pieces, act))
    grad_gate, grad_up, dy_all, sent_down, sent_gate, sent_up = on_core(
        functools.partial(turn_body, len(wd_pieces)),
        [shape((T, H), BF)] * 2 + [shape((T, D), BF), shape((H, DH), BF)] + [shape((DH, H), BF)] * 2,
        [pltpu.VMEM((H, D), BF)],
    )(*dy_parts, *wd_pieces, slope, silu, act, normed2)
    got_down, got_gate, got_up = near(sent_down, sent_gate, sent_up)
    gn2_own, t1, t2, t3, norm2_part = on_core(
        functools.partial(through_body, len(wg_pieces)),
        [shape((Q, D), F32)] + [shape((Q, D), BF)] * 3 + [shape((1, D), F32)],
        [pltpu.VMEM((D, 2 * H), BF)],
    )(*wg_pieces, grad_gate, grad_up, xhat2)
    t1, t2, t3, got_down, got_gate, got_up = join((t1, t2, t3, got_down, got_gate, got_up))

    def keep(body, mine, left, right, got):
        return on_core(functools.partial(body, twin), [shape(mine, F32), shape(mine, BF)])(left, right, got)

    def add_far(mine, got):
        return low(mine + got.astype(F32))

    def add_dp(mine):
        if twin:
            return mine.astype(F32) + over(mine).astype(F32)
        return lax.psum(mine.astype(F32), "dp")

    gn2_got = [swap(t, "rows", k) for k, t in ((2, t2), (3, t3), (1, t1))]
    down_mine, down_far = keep(keep_cols_body, (H, F), act, dy_all, got_down)
    down_far = swap(down_far, "cols", 2)
    gate_mine, gate_far = keep(keep_rows_body, (F, H), normed2, grad_gate, got_gate)
    up_mine, up_far = keep(keep_rows_body, (F, H), normed2, grad_up, got_up)
    gn2_got, down_far, gate_far, up_far = join((gn2_got, down_far, gate_far, up_far))
    for g in gn2_got:
        gn2_own = gn2_own + g.astype(F32)
    down = add_far(down_mine, down_far)

    inv2_own = lax.rsqrt(jnp.mean(mid_own * mid_own, axis=1, keepdims=True) + EPS)
    scaled = gn2_own * gains[1:2]
    inner = jnp.mean(scaled * mid_own, axis=1, keepdims=True)
    grad_mid = dy_own.astype(F32) + inv2_own * scaled - mid_own * (inv2_own**3 * inner)

    gm_low, gate_far, up_far, down = join((grad_mid.astype(BF), gate_far, up_far, down))
    gm_parts = gather_rows(gm_low)
    gate_far = swap(gate_far, "cols", 2)
    up_far = jnp.split(up_far, 2, axis=0)
    up_first = swap(up_far[0], "cols", 2)
    down_grad = add_dp(down)
    gm_parts, gate_far, up_first, down_grad = join((gm_parts, gate_far, up_first, down_grad))
    gate = add_far(gate_mine, gate_far)
    up_a = add_far(up_mine[:half], up_first)

    gproj, gm_all, xhat1, sent_out, sent_in, kernel_part = on_core(
        functools.partial(back_body, len(wo_pieces), twin),
        [shape((TE, 3 * W), BF), shape((T, D), BF), shape((TE, D), F32), shape((W, DH), BF), shape((DH, 3 * W), BF)]
        + [shape((3, W), F32)],
        [pltpu.VMEM((R, EDGE, W), F32), pltpu.VMEM((R, EDGE, W), F32), pltpu.VMEM((W, D), BF)],
    )(lengths, *gm_parts, *[w[:W] for w in wo_pieces], *x_parts, kernel, proj, mixin, normed1, scalars=1)
    got_out, got_in = near(sent_out, sent_in)
    gn1_own, t1, t2, t3, norm1_part = on_core(
        functools.partial(last_body, len(wi_pieces)),
        [shape((E, D), F32)] + [shape((E, D), BF)] * 3 + [shape((1, D), F32)],
        [pltpu.VMEM((D, 3 * W), BF)],
    )(*wi_pieces, gproj, xhat1)

    t1, t2, t3, got_out, got_in, up_last, gate, up_a = join((t1, t2, t3, got_out, got_in, up_far[1], gate, up_a))
    gn1_got = [swap(t, "rows", k) for k, t in ((2, t2), (3, t3), (1, t1))]
    up_last = swap(up_last, "cols", 2)
    in_mine, in_far = keep(keep_rows_body, (F, 3 * W), normed1, gproj, got_in)
    out_mine, out_far = keep(keep_cols_body, (W, F), mixin, gm_all, got_out)
    in_far = swap(in_far, "cols", 2)
    out_far = swap(out_far, "cols", 2)
    gate_grad = add_dp(gate)
    up_a_grad = add_dp(up_a)
    gn1_got, up_last, in_far, out_far, gate_grad, up_a_grad = join(
        (gn1_got, up_last, in_far, out_far, gate_grad, up_a_grad)
    )
    for g in gn1_got:
        gn1_own = gn1_own + g.astype(F32)

    up_b_grad = add_dp(add_far(up_mine[half:], up_last))
    in_grad = add_dp(add_far(in_mine, in_far)).reshape(F, 3, W)
    out_grad = add_dp(add_far(out_mine, out_far))
    gu_grad = jnp.stack([gate_grad, cat([up_a_grad, up_b_grad], 0)], axis=1)

    wd_a, wd_b = wd_pieces[: len(wd_pieces) // 2], wd_pieces[len(wd_pieces) // 2 :]
    act_late = after(act, gn1_own)
    out = cat([dot(act_late, cat(wd_a, 1)), dot(act_late, cat(wd_b, 1))], 1)
    out_own = mid_own + scatter_rows(out[:Q], [low(out[k * Q : (k + 1) * Q]) for k in range(1, R)])

    x_own_f = x_own.astype(F32)
    inv1_own = lax.rsqrt(jnp.mean(x_own_f * x_own_f, axis=1, keepdims=True) + EPS)
    scaled1 = gn1_own * gains[0:1]
    inner1 = jnp.mean(scaled1 * x_own_f, axis=1, keepdims=True)
    input_own = inv1_own * scaled1 - x_own_f * (inv1_own**3 * inner1)
    input_own = input_own + cat([grad_mid, jnp.zeros((EDGE, D), F32)], 0)

    def to_shard(a, send):
        blocks = [a[:, i * F : (i + 1) * F] for i in range(C)]
        by_k = [blocks[order.index(k)] for k in range(C)]
        by_k = [by_k[0]] + [swap(send(b if k < 2 else flip(b, 1)), "cols", k) for k, b in enumerate(by_k) if k]
        return pick([b.astype(F32) for b in by_k], [c ^ i for i in range(C)])

    block_output = cat(to_shard(out_own.astype(BF), lambda b: b), 0).astype(BF)
    got = to_shard(input_own, low)
    rows = []
    for i in range(C):
        later = got[(i + 1) % C][Q:]
        rows += [got[i][: Q - EDGE], got[i][Q - EDGE : Q] + later]
    input_grad = cat(rows, 0)

    n1 = norm1_part.reshape(C, F)
    n2 = norm2_part.reshape(C, F)
    small = cat([n1[:2], n2[:2], kernel_part], 0) + swap(cat([n1[2:], n2[2:], kernel_part], 0), "cols", 1)
    theirs = cat([flip(small[1:2], 1), flip(small[3:4], 1), small[4:]], 0)
    small = cat([small[0:1], small[2:3], small[4:]], 0) + swap(theirs, "cols", 2)
    if twin:
        small = small + swap(small, "dp", 1)
    else:
        small = lax.psum(small, "dp")
    norms = small[:2]
    for bit in (1, 2):
        norms = norms + swap(norms, "rows", bit)
    return (
        block_output,
        input_grad,
        norms[0],
        in_grad,
        small[2:],
        out_grad,
        norms[1],
        gu_grad,
        down_grad,
    )


def solution(mesh):
    tok = P(("dp", "rows"), "cols")
    feat = P("cols")
    wide = P("cols", None, "rows")
    tall = P("rows", "cols")
    taps = P(None, "rows")
    return jax.shard_map(
        local,
        mesh=mesh,
        in_specs=(tok, P("dp", None), feat, wide, taps, tall, feat, wide, tall, tok),
        out_specs=(tok, tok, feat, wide, taps, tall, feat, wide, tall),
        check_vma=False,
    )
```

```python
import jax
import jax.numpy as jnp
from jax import lax
from jax.experimental import pallas as pl
from jax.experimental.pallas import tpu as pltpu
from jax.sharding import PartitionSpec as P

EPS = 1e-06
BF = jnp.bfloat16
F32 = jnp.float32
EDGE = 8


def swap(value, axis, bit):
    size = lax.axis_size(axis)
    return lax.ppermute(value, axis, [(i, i ^ bit) for i in range(size)])


def dot(a, b):
    return jnp.dot(a, b, preferred_element_type=F32)


def dot_t(a, b):
    return lax.dot_general(a, b, (((1,), (1,)), ((), ())), preferred_element_type=F32)


def t_dot(a, b):
    return lax.dot_general(a, b, (((0,), (0,)), ((), ())), preferred_element_type=F32)


def low(v):
    return lax.reduce_precision(v, 8, 7).astype(BF)


def after(value, *first):
    return lax.optimization_barrier((value,) + first)[0]


def cat(parts, dim):
    return jnp.concatenate(parts, axis=dim)


def on_core(body, out, scratch=(), copies=0, limit=24):
    vmem, away = pl.BlockSpec(memory_space=pltpu.VMEM), pl.BlockSpec(memory_space=pltpu.HBM)

    def call(scalars, far, near):
        return pl.pallas_call(
            body,
            out_shape=[o[0] if isinstance(o, tuple) else o for o in out],
            in_specs=[pl.BlockSpec(memory_space=pltpu.SMEM)] * len(scalars)
            + [away] * len(far)
            + [vmem] * len(near),
            out_specs=[away if isinstance(o, tuple) else vmem for o in out],
            scratch_shapes=list(scratch) + ([pltpu.SemaphoreType.DMA((copies,))] if copies else []),
            compiler_params=pltpu.CompilerParams(vmem_limit_bytes=limit * 2**20),
            cost_estimate=pl.CostEstimate(flops=0, bytes_accessed=2**16, transcendentals=0),
        )(*scalars, *far, *near)

    return call


def pull(pairs, sems, first=0):
    started = []
    for i, (source, target) in enumerate(pairs):
        copy = pltpu.make_async_copy(source, target, sems.at[first + i])
        copy.start()
        started.append(copy)
    return started


def arrived(copies):
    for copy in copies:
        copy.wait()


def laid(target, pieces, dim):
    pairs, at = [], 0
    for piece in pieces:
        size = piece.shape[dim]
        place = target.at[pl.ds(at, size), :] if dim == 0 else target.at[:, pl.ds(at, size)]
        pairs.append((piece, place))
        at += size
    return pairs


def shape(dims, kind):
    return jax.ShapeDtypeStruct(dims, kind)


def stored(dims, kind):
    return (shape(dims, kind),)


def place_body(tokens, cotangent, gain1, gain2, p0, p1, p2, p3, edges, gains, sems):
    S = tokens.shape[0]
    Q = S // 4
    mine = Q + 2 * EDGE
    c = lax.axis_index("cols")
    outs = (p0, p1, p2, p3)
    soon = [(gain1, gains.at[0]), (gain2, gains.at[1])]
    later = []
    for k in range(4):
        start = pl.multiple_of((c ^ k) * Q, 16)
        early = pl.multiple_of(lax.rem(start + S - 16, S), 16)
        soon.append((tokens.at[pl.ds(early, 16), :], edges.at[k]))
        later.append((tokens.at[pl.ds(start, Q), :], outs[k].at[pl.ds(0, Q), :]))
        later.append((cotangent.at[pl.ds(start, Q), :], outs[k].at[pl.ds(mine, Q), :]))
    soon = pull(soon, sems)
    later = pull(later, sems, len(soon))
    arrived(soon)
    rows = lax.broadcasted_iota(jnp.int32, (EDGE, tokens.shape[1]), 0)
    values = jnp.zeros(rows.shape, F32)
    at = 0
    for i in range(2):
        left = gains[i]
        for _ in range(3):
            part = left.astype(BF).astype(F32)
            left = left - part
            values = jnp.where(rows == at, part, values)
            at += 1
    for k in range(4):
        edge = edges[k].astype(F32)[16 - EDGE :]
        outs[k][Q:mine, :] = jnp.concatenate([edge, values], axis=0).astype(BF)
    arrived(later)


def join_body(p0, p2, p1, p3, x_ref, dy_ref, g_ref, held, sems):
    F = p0.shape[1]
    Q = dy_ref.shape[0]
    copies = pull([(p, held.at[i]) for i, p in enumerate((p0, p2, p1, p3))], sems)
    for i, copy in enumerate(copies):
        copy.wait()
        cols = slice(i * F, (i + 1) * F)
        x_ref[:, cols] = held[i, : Q + 2 * EDGE]
        dy_ref[:, cols] = held[i, Q + 2 * EDGE :]
        t = held[i, Q : Q + 2 * EDGE].astype(F32)[EDGE:]
        g_ref[0:1, cols] = (t[0:1] + t[1:2]) + t[2:3]
        g_ref[1:2, cols] = (t[3:4] + t[4:5]) + t[5:6]


def chunk_taps(lengths, j, S, Q, W):
    z, c = lax.axis_index("rows"), lax.axis_index("cols")
    place = (z ^ j) * S + c * Q + lax.broadcasted_iota(jnp.int32, (Q, W), 0)
    end = jnp.int32(0)
    start = jnp.zeros_like(place)
    for i in range(lengths.shape[1]):
        end = end + lengths[0, i]
        start = jnp.where(place >= end, end, start)
    return [jnp.logical_and(place < end, place - start >= lag) for lag in range(3)]


def neighbour(j):
    z, c = lax.axis_index("rows"), lax.axis_index("cols")
    return jnp.where(c == 0, lax.rem((z ^ j) + 3, 4) ^ z, j)


def edge_products(proj_ref, edges, T, W):
    for j in range(4):
        lo = T + j * EDGE
        edges[j] = (proj_ref[lo : lo + EDGE, :W] * proj_ref[lo : lo + EDGE, 2 * W :]).astype(BF).astype(F32)


def tapped_lags(proj_ref, edges, taps, j, Q, W):
    lo = j * Q
    bv = (proj_ref[lo : lo + Q, :W] * proj_ref[lo : lo + Q, 2 * W :]).astype(BF).astype(F32)
    edge = edges[neighbour(j)]
    row = lax.broadcasted_iota(jnp.int32, (Q, W), 0)
    one = jnp.where(row == 0, edge[EDGE - 1 :], pltpu.roll(bv, 1, 0))
    two = pltpu.roll(bv, 2, 0)
    two = jnp.where(row == 0, edge[EDGE - 2 : EDGE - 1], jnp.where(row == 1, edge[EDGE - 1 :], two))
    return [jnp.where(tap, lagged, 0.0) for tap, lagged in zip(taps, (bv, one, two))]


def blocks_of(target, gathered):
    c = lax.axis_index("cols")
    size = gathered.shape[0] // 4
    pairs = []
    for i, k in enumerate((0, 2, 1, 3)):
        place = target.at[pl.ds(i * size, size), :]
        start = pl.multiple_of((c ^ k) * size, 16)
        pairs.append((gathered.at[pl.ds(start, size), :], place))
    return pairs


def split(refs, *counts):
    out = []
    for n in counts:
        out.append(refs[:n])
        refs = refs[n:]
    return out + [refs]


def mixer_body(lengths, r0, r1, r2, r3, kernel_in, w_in, gain, *refs):
    outs, (normed, proj, mixin, xs, w, edges, kernel, sems) = split(refs, 3)
    Q = xs.shape[1] - 2 * EDGE
    T = 4 * Q
    W = kernel.shape[1]
    tokens = pull([(r, xs.at[j]) for j, r in enumerate((r0, r1, r2, r3))], sems)
    tokens += pull([(kernel_in, kernel)], sems, 4)
    weights = pull(blocks_of(w, w_in), sems, 5)
    tail = []
    for j in range(4):
        tokens[j].wait()
        v = xs[j, : Q + EDGE, :].astype(F32)
        inv = lax.rsqrt(jnp.mean(v * v, axis=1, keepdims=True) + EPS)
        n = v * inv * gain[0:1, :]
        normed[j * Q : (j + 1) * Q, :] = n[:Q].astype(BF)
        tail.append(n[Q:])
    normed[T:, :] = jnp.concatenate(tail, axis=0).astype(BF)
    out = pull([(normed, outs[0])], sems, 9)
    arrived(weights + tokens[4:])
    for i in range(3):
        cols = slice(i * W, (i + 1) * W)
        proj[:, cols] = dot(normed[...], w[:, cols])
    out += pull([(proj, outs[1])], sems, 10)
    edge_products(proj, edges, T, W)
    for j in range(4):
        taps = chunk_taps(lengths, j, 4 * Q, Q, W)
        lags = tapped_lags(proj, edges, taps, j, Q, W)
        conv = kernel[0:1, :] * lags[0] + kernel[1:2, :] * lags[1] + kernel[2:3, :] * lags[2]
        rows = slice(j * Q, (j + 1) * Q)
        mixin[rows, :] = (proj[rows, W : 2 * W] * conv).astype(BF)
        out += pull([(mixin.at[pl.ds(j * Q, Q), :], outs[2].at[pl.ds(j * Q, Q), :])], sems, 11 + j)
    arrived(out)


def hidden_tiles(H):
    return [(h, min(256, H - h)) for h in range(0, H, 256)]


def forward_body(*refs):
    rs, ms, wos, wgs, (gain,), rest = split(refs, 4, 4, 4, 4, 1)
    mid_own, normed, xhat, act, slope, silu_ref, wg, xs, mid, mix, wo, sems = rest
    T, W = ms[0].shape
    Q = T // 4
    H = act.shape[1]
    gain2 = gain[1:2, :]
    tokens = [(r.at[pl.ds(0, Q), :], xs.at[j]) for j, r in enumerate(rs)]
    blocks = [
        (ms[k].at[pl.ds((j ^ k) * Q, Q), :], mix.at[pl.ds(j * Q, Q), pl.ds(k * W, W)])
        for j in range(4)
        for k in range(4)
    ]
    outs = pull(laid(wo, wos, 1), sems)
    blocks = pull(blocks, sems, 4)
    tokens = pull(tokens, sems, 20)
    wide = pull(laid(wg, wgs, 0), sems, 24)
    arrived(outs)
    for j in range(4):
        arrived(blocks[4 * j : 4 * j + 4])
        tokens[j].wait()
        rows = slice(j * Q, (j + 1) * Q)
        mid[rows, :] = xs[j].astype(F32) + dot(mix[rows, :], wo[...])
        v = mid[rows, :]
        inv = lax.rsqrt(jnp.mean(v * v, axis=1, keepdims=True) + EPS)
        xhat[rows, :] = v * inv
        normed[rows, :] = (v * inv * gain2).astype(BF)
    mid_own[...] = mid[:Q, :]
    arrived(wide)
    for h, size in hidden_tiles(H):
        cols, ups = slice(h, h + size), slice(H + h, H + h + size)
        gate = dot(normed[...], wg[:, cols])
        up = dot(normed[...], wg[:, ups])
        sig = 1.0 / (1.0 + jnp.exp(-gate))
        silu = gate * sig
        act[:, cols] = (silu * up).astype(BF)
        silu_ref[:, cols] = silu
        slope[:, cols] = up * sig * (1.0 + gate * (1.0 - sig))


def out_body(w0, w1, w2, w3, act, own, s1, s2, s3, wd, sems):
    Q, D = own.shape
    copies = pull(laid(wd, (w0, w1, w2, w3), 1), sems)
    for i, n in enumerate(range(0, D, D // 4)):
        cols = slice(n, n + D // 4)
        copies[i].wait()
        v = dot(act[...], wd[:, cols])
        own[:, cols] = v[:Q]
        for k, out in ((1, s1), (2, s2), (3, s3)):
            out[:, cols] = v[k * Q : (k + 1) * Q].astype(BF)


def turn_body(r0, r1, r2, r3, wd, slope, silu, act, normed, gg, gu, dy_all, sent1, sent2, sems):
    T, D = dy_all.shape
    H = act.shape[1]
    Q = T // 4
    F = D // 4
    half = F // 2
    arrived(pull(laid(dy_all, (r0, r1, r2, r3), 0), sems))
    for h, size in hidden_tiles(H):
        cols = slice(h, h + size)
        grad = dot_t(dy_all[...], wd[cols, :])
        gu[:, cols] = (grad * silu[:, cols]).astype(BF)
        gg[:, cols] = (grad * slope[:, cols]).astype(BF)
        for i in range(2):
            at, to = (2 + i) * F, 3 * half * i
            sent1[to : to + F, cols] = t_dot(dy_all[:, at : at + F], act[:, cols]).astype(BF)
            v = t_dot(normed[:, at : at + F], gg[:, cols]).astype(BF)
            sent1[to + F : to + 3 * half, cols] = v[:half]
            sent2[to : to + half, cols] = v[half:]
            sent2[to + half : to + 3 * half, cols] = t_dot(normed[:, at : at + F], gu[:, cols]).astype(BF)


def through_body(wg, gg, gu, xhat, own, s1, s2, s3, norm_part):
    Q, D = own.shape
    H = gg.shape[1]
    for n in range(0, D, D // 4):
        cols = slice(n, n + D // 4)
        v = dot_t(gg[...], wg[cols, :H]) + dot_t(gu[...], wg[cols, H:])
        norm_part[0:1, cols] = jnp.sum(v * xhat[:, cols], axis=0, keepdims=True)
        own[:, cols] = v[:Q]
        for k, out in ((1, s1), (2, s2), (3, s3)):
            out[:, cols] = v[k * Q : (k + 1) * Q].astype(BF)


def keep1_body(got_in, dy_all, act, normed, gg, mine, theirs, got, sems):
    rows = mine.shape[0]
    F = 2 * rows // 3
    half = F // 2
    H = act.shape[1]
    arrived(pull([(got_in, got)], sems))
    for i, out in enumerate((mine, theirs)):
        for h, size in hidden_tiles(H):
            cols = slice(h, h + size)
            v = t_dot(dy_all[:, i * F : (i + 1) * F], act[:, cols]) + got[i * rows : i * rows + F, cols].astype(F32)
            out[:F, cols] = v.astype(out.dtype)
            v = t_dot(normed[:, i * F : i * F + half], gg[:, cols]) + got[i * rows + F : (i + 1) * rows, cols].astype(F32)
            out[F:, cols] = v.astype(out.dtype)


def keep2_body(got_in, normed, gg, gu, mine, theirs, got, sems):
    rows = mine.shape[0]
    F = 2 * rows // 3
    half = F // 2
    H = gg.shape[1]
    arrived(pull([(got_in, got)], sems))
    for i, out in enumerate((mine, theirs)):
        for h, size in hidden_tiles(H):
            cols = slice(h, h + size)
            at = i * rows
            v = t_dot(normed[:, i * F + half : (i + 1) * F], gg[:, cols]) + got[at : at + half, cols].astype(F32)
            out[:half, cols] = v.astype(out.dtype)
            v = t_dot(normed[:, i * F : (i + 1) * F], gu[:, cols]) + got[at + half : at + rows, cols].astype(F32)
            out[half:, cols] = v.astype(out.dtype)


def keep3_body(got_in, normed, gproj, gm_all, mixin, mine, theirs, got, sems):
    F = mine.shape[0]
    W = mixin.shape[1]
    arrived(pull([(got_in, got)], sems))
    for i, out in enumerate((mine, theirs)):
        rows = slice(i * F, (i + 1) * F)
        for n in range(3):
            cols = slice(n * W, (n + 1) * W)
            out[:, cols] = (t_dot(normed[:, rows], gproj[:, cols]) + got[rows, cols].astype(F32)).astype(out.dtype)
        cols = slice(3 * W, 4 * W)
        out[:, cols] = (t_dot(gm_all[:, rows], mixin[...]) + got[rows, cols].astype(F32)).astype(out.dtype)


def back_body(lengths, *refs):
    gms, rs, wos, (w_in, kernel_in, proj_in, mixin_in, normed_in), rest = split(refs, 4, 4, 4, 5)
    gproj, gm_all, xhat, sent, kernel_part, mixin, normed, wi, edges, back, wo, kernel, xs, proj, sems = rest
    Q = gms[0].shape[0]
    T = 4 * Q
    W = kernel.shape[1]
    DH = wo.shape[1] // 2
    row = lax.broadcasted_iota(jnp.int32, (Q, W), 0)
    soon = pull([(proj_in, proj)], sems)
    tokens = pull([(r, xs.at[j]) for j, r in enumerate(rs)], sems, 1)
    copies = pull(
        laid(gm_all, gms, 0)
        + laid(wo, [w.at[pl.ds(0, W), :] for w in wos], 1)
        + [(kernel_in, kernel), (mixin_in, mixin), (normed_in, normed)],
        sems,
        5,
    )
    weights = pull(blocks_of(wi, w_in), sems, 16)
    arrived(soon)
    edge_products(proj, edges, T, W)
    back[...] = jnp.zeros(back.shape, F32)
    arrived(copies)
    sums = [jnp.zeros((1, W), F32)] * 3
    tail = []
    for j in range(4):
        rows = slice(j * Q, (j + 1) * Q)
        grad_mix = dot_t(gm_all[rows, :], wo[...])
        taps = chunk_taps(lengths, j, 4 * Q, Q, W)
        lags = tapped_lags(proj, edges, taps, j, Q, W)
        conv = kernel[0:1, :] * lags[0] + kernel[1:2, :] * lags[1] + kernel[2:3, :] * lags[2]
        grad_conv = (grad_mix * proj[rows, W : 2 * W]).astype(BF).astype(F32)
        sums = [s + jnp.sum(grad_conv * lag, axis=0, keepdims=True) for s, lag in zip(sums, lags)]
        m0, m1, m2 = [jnp.where(tap, grad_conv, 0.0) for tap in taps]
        m1 = kernel[1:2, :] * m1
        m2 = kernel[2:3, :] * m2
        grad_bv = kernel[0:1, :] * m0
        grad_bv = grad_bv + jnp.where(row < Q - 1, pltpu.roll(m1, Q - 1, 0), 0.0)
        grad_bv = grad_bv + jnp.where(row < Q - 2, pltpu.roll(m2, Q - 2, 0), 0.0)
        head = lax.broadcasted_iota(jnp.int32, (EDGE, W), 0)
        last = jnp.where(head == EDGE - 1, m1[0:1] + m2[1:2], 0.0)
        back[neighbour(j)] = jnp.where(head == EDGE - 2, m2[0:1], last)
        gproj[rows, :W] = (grad_bv * proj[rows, 2 * W :]).astype(BF)
        gproj[rows, W : 2 * W] = (grad_mix * conv).astype(BF)
        gproj[rows, 2 * W :] = (grad_bv * proj[rows, :W]).astype(BF)
    for i in range(3):
        kernel_part[i : i + 1, :] = sums[i]
    for j in range(4):
        lo = T + j * EDGE
        tail.append(
            jnp.concatenate(
                [back[j] * proj[lo : lo + EDGE, 2 * W :], jnp.zeros((EDGE, W), F32), back[j] * proj[lo : lo + EDGE, :W]],
                axis=1,
            )
        )
    gproj[T:, :] = jnp.concatenate(tail, axis=0).astype(BF)
    for i in range(3):
        cols = slice(i * W, (i + 1) * W)
        sent[:, cols] = t_dot(normed[:, DH:], gproj[:, cols]).astype(BF)
    sent[:, 3 * W :] = t_dot(gm_all[:, DH:], mixin[...]).astype(BF)
    for j in range(4):
        tokens[j].wait()
        v = xs[j, : Q + EDGE, :].astype(F32)
        v = v * lax.rsqrt(jnp.mean(v * v, axis=1, keepdims=True) + EPS)
        xhat[j * Q : (j + 1) * Q, :] = v[:Q]
        xhat[T + j * EDGE : T + (j + 1) * EDGE, :] = v[Q:]
    arrived(weights)


def last_body(w, gproj, xhat, norm2, own, s1, s2, s3, norms):
    D = own.shape[1]
    Q = own.shape[0] - 2 * EDGE
    T = 4 * Q
    head = lax.broadcasted_iota(jnp.int32, (EDGE, D // 4), 0)
    for n in range(0, D, D // 4):
        cols = slice(n, n + D // 4)
        v = dot_t(gproj[...], w[cols, :])
        one = jnp.sum(v * xhat[:, cols], axis=0, keepdims=True).astype(BF).astype(F32)
        two = norm2[:, cols].astype(BF).astype(F32)
        norms[0:1, cols] = one
        norms[1:2, cols] = two
        more = jnp.where(head == 0, one, jnp.where(head == 1, two, 0.0))
        for k, out in enumerate((own, s1, s2, s3)):
            out[:Q, cols] = v[k * Q : (k + 1) * Q].astype(out.dtype)
            edge = v[T + k * EDGE : T + (k + 1) * EDGE]
            out[Q:, cols] = jnp.concatenate([edge, more], axis=0).astype(out.dtype)


def finish_body(g2, g3, g1, o2, o3, o1, own, x_own, gain, grad_mid, mid_own, out_own, norms, kernel_part, p0, p2, p1, p3, got, got_out, sems):
    Q, D = out_own.shape
    E = Q + EDGE
    F = D // 4
    copies = pull([(g, got.at[i]) for i, g in enumerate((g2, g3, g1))], sems)
    outer = pull([(o, got_out.at[i]) for i, o in enumerate((o2, o3, o1))], sems, 3)
    x = x_own[...].astype(F32)[:E]
    inv = lax.rsqrt(jnp.mean(x * x, axis=1, keepdims=True) + EPS)
    arrived(copies)
    two, three, one = [got[i].astype(F32) for i in range(3)]
    total = (norms[...] + one[E : E + 2]) + (two[E : E + 2] + three[E : E + 2])
    grad = own[:E, :] + two[:E] + three[:E] + one[:E]
    scaled = grad * gain[0:1, :]
    inner = jnp.mean(scaled * x, axis=1, keepdims=True)
    res = inv * scaled - x * (inv * inv * inv * inner)
    arrived(outer)
    out = mid_own[...] + out_own[...]
    for i in range(3):
        out = out + got_out[i].astype(F32)
    main = res[:Q] + grad_mid[...]
    small = jnp.concatenate([total, jnp.zeros((EDGE - 2, D), F32)], axis=0)
    row = lax.broadcasted_iota(jnp.int32, (EDGE, F), 0)
    for i, piece in enumerate((p0, p2, p1, p3)):
        cols = slice(i * F, (i + 1) * F)
        sums = small[:, cols]
        for n in range(3):
            sums = jnp.where(row == 2 + n, kernel_part[n : n + 1, :], sums)
        edge = jnp.concatenate([res[Q:, cols], sums], axis=0)
        piece[:Q, :] = main[:, cols].astype(BF)
        piece[Q : Q + 2 * EDGE, :] = edge.astype(BF)
        piece[Q + 2 * EDGE :, :] = out[:, cols].astype(BF)


def settle_body(p0, p1, p2, p3, grad_ref, out_ref, small, held, sems):
    S = grad_ref.shape[0]
    Q = S // 4
    c = lax.axis_index("cols")
    copies = pull([(p, held.at[k]) for k, p in enumerate((p0, p1, p2, p3))], sems)
    arrived(copies)
    for k in range(4):
        start = pl.multiple_of((c ^ k) * Q, 16)
        grad_ref[pl.ds(start, Q), :] = held[k, :Q].astype(F32)
        out_ref[pl.ds(start, Q), :] = held[k, Q + 2 * EDGE :]
    for k in range(4):
        before = pl.multiple_of(lax.rem((c ^ k) * Q + S - EDGE, S), 8)
        grad_ref[pl.ds(before, EDGE), :] += held[k, Q : Q + 2 * EDGE].astype(F32)[:EDGE]
    s0, s1, s2, s3 = [held[k, Q : Q + 2 * EDGE].astype(F32)[EDGE:] for k in range(4)]
    small[...] = (s0 + s1) + (s2 + s3)


def local(tokens, lengths, gain1, w_in, kernel, w_out, gain2, w_gu, w_down, cotangent):
    S, F = tokens.shape
    R, C = lax.axis_size("rows"), lax.axis_size("cols")
    assert R == 4 and C == 4
    y = lax.axis_index("dp")
    twin = lax.axis_size("dp") == 2
    Q = S // C
    E = Q + EDGE
    T = R * Q
    TE = R * E
    W = w_out.shape[0]
    H = w_down.shape[0]
    D = C * F
    DH = 2 * F
    half = F // 2

    order = (0, 2, 1, 3)

    def exchange(pieces):
        return [pieces[0]] + [swap(pieces[k], "cols", k) for k in (1, 2, 3)]

    def gather_rows(a):
        far_two = swap(a, "rows", 2)
        far_three = swap(a, "rows", 3)
        return [a, swap(a, "rows", 1), far_two, far_three]

    def over(v):
        return swap(v, "dp", 1)

    def near(*vs):
        return [swap(v, "cols", 1) for v in vs]

    join = lax.optimization_barrier
    vmem = pltpu.VMEM
    mine = E + EDGE

    placed = on_core(
        place_body, [shape((mine + Q, F), BF)] * 4, [vmem((R, 16, F), BF), vmem((2, 1, F), F32)], 14, 60
    )((), (tokens, cotangent, gain1.reshape(1, F), gain2.reshape(1, F)), ())
    pieces = exchange(placed)
    wi_all = lax.all_gather(w_in.reshape(F, 3 * W), "cols", tiled=True)
    wo = after(w_out, placed[0])
    if twin:
        wo = jnp.where(y == 0, wo[:, : F // 2], wo[:, F // 2 :])
    pieces, wo_parts = join((pieces, gather_rows(wo)))
    x_own, dy_own, gains = on_core(
        join_body,
        [shape((mine, D), BF), shape((Q, D), BF), shape((2, D), F32)],
        [vmem((C, mine + Q, F), BF)],
        4,
    )((), [pieces[k] for k in order], ())

    wg = after(w_gu, x_own).reshape(F, 2 * H)
    parts = gather_rows(x_own)
    wo = cat(wo_parts, 0)
    if twin:
        wo_other = swap(wo, "dp", 1)
        wo = cat([jnp.where(y == 0, wo, wo_other), jnp.where(y == 0, wo_other, wo)], 1)
    wg_far = swap(wg, "cols", 2)
    parts = join(parts)
    normed1, proj, mixin = on_core(
        mixer_body,
        [stored((TE, D), BF), stored((TE, 3 * W), F32), stored((T, W), BF)],
        [vmem((TE, D), BF), vmem((TE, 3 * W), F32), vmem((T, W), BF), vmem((R, mine, D), BF), vmem((D, 3 * W), BF)]
        + [vmem((R, EDGE, W), F32), vmem((3, W), F32)],
        15,
        60,
    )((lengths,), (*parts, kernel, wi_all), (gains,))

    mixin, wg_far, wo = join((mixin, wg_far, wo))
    mix_parts = gather_rows(mixin)
    wo_far = swap(wo, "cols", 2)
    wd = after(w_down, wg_far)
    wd_far = swap(wd, "cols", 2)
    wo_near, wg_near, wg_last, wd_near = near(wo, wg, wg_far, wd)
    mix_parts, wo_far, wd_far, wo_near, wg_near, wg_last, wd_near = join(
        (mix_parts, wo_far, wd_far, wo_near, wg_near, wg_last, wd_near)
    )
    wg_pieces = [wg, wg_far, wg_near, wg_last]
    wo_pieces = [wo, wo_far, wo_near, swap(wo_far, "cols", 1)]

    dy_parts = gather_rows(after(dy_own, mix_parts[1]))
    mid_own, normed2, xhat2, act, slope, silu, wg_here = on_core(
        forward_body,
        [shape((Q, D), F32), shape((T, D), BF), shape((T, D), F32), shape((T, H), BF), shape((T, H), F32), shape((T, H), F32)]
        + [shape((D, 2 * H), BF)],
        [vmem((R, Q, D), BF), vmem((T, D), F32), vmem((T, D), BF), vmem((D, D), BF)],
        28,
    )((), (*parts, *mix_parts, *wo_pieces, *wg_pieces), (gains,))
    wd_pieces = [wd, wd_far, wd_near, swap(wd_far, "cols", 1)]
    out_own, o1, o2, o3, wd_here = on_core(
        out_body, [shape((Q, D), F32)] + [shape((Q, D), BF)] * 3 + [shape((H, D), BF)], (), 4
    )((), wd_pieces, (act,))
    dy_parts, o1, o2, o3, wd_here = join((dy_parts, o1, o2, o3, wd_here))

    out_got = [swap(o2, "rows", 2)]
    grad_gate, grad_up, dy_all, sent1, sent2 = on_core(
        turn_body,
        [shape((T, H), BF)] * 2 + [shape((T, D), BF)] + [shape((3 * F, H), BF)] * 2,
        (),
        4,
    )((), dy_parts, (wd_here, slope, silu, act, normed2))
    got1, got2 = near(sent1, sent2)
    gn2_own, t1, t2, t3, norm2_part = on_core(
        through_body, [shape((Q, D), F32)] + [shape((Q, D), BF)] * 3 + [shape((1, D), F32)]
    )((), (), (wg_here, grad_gate, grad_up, xhat2))
    def keep(body, size, got, *arrays):
        return on_core(body, [shape(size, F32), shape(size, BF)], [vmem(got.shape, BF)], 1)((), (got,), arrays)

    def add_far(mine, got):
        return low(mine + got.astype(F32))

    def add_dp(mine, other):
        if twin:
            return mine.astype(F32) + other.astype(F32)
        return lax.psum(mine.astype(F32), "dp")

    def over(v):
        return swap(v, "dp", 1) if twin else v

    third = 3 * half
    mine1, far1 = keep(keep1_body, (third, H), got1, dy_all, act, normed2, grad_gate)
    t1, t2, t3, mine1, far1, got2, out_got = join((t1, t2, t3, mine1, far1, got2, out_got))

    gn2_got = [swap(t, "rows", k) for k, t in ((2, t2), (3, t3), (1, t1))]
    far1 = swap(far1, "cols", 2)
    mine2, far2 = keep(keep2_body, (third, H), got2, normed2, grad_gate, grad_up)
    gn2_got, far1, far2 = join((gn2_got, far1, far2))
    for g in gn2_got:
        gn2_own = gn2_own + g.astype(F32)
    inv2_own = lax.rsqrt(jnp.mean(mid_own * mid_own, axis=1, keepdims=True) + EPS)
    scaled = gn2_own * gains[1:2]
    inner = jnp.mean(scaled * mid_own, axis=1, keepdims=True)
    grad_mid = dy_own.astype(F32) + inv2_own * scaled - mid_own * (inv2_own**3 * inner)
    sum1 = add_far(mine1, far1)

    gm_low, far2, sum1 = join((grad_mid.astype(BF), far2, sum1))
    gm_parts = gather_rows(gm_low)
    far2 = swap(far2, "cols", 2)
    other1 = over(sum1)
    gm_parts, far2, other1 = join((gm_parts, far2, other1))
    sum2 = add_far(mine2, far2)
    gproj, gm_all, xhat1, sent3, kernel_part, mixin_here, normed_here, wi_here = on_core(
        back_body,
        [shape((TE, 3 * W), BF), shape((T, D), BF), shape((TE, D), F32), shape((DH, 4 * W), BF), shape((3, W), F32)]
        + [shape((T, W), BF), shape((TE, D), BF), shape((D, 3 * W), BF)],
        [vmem((R, EDGE, W), F32), vmem((R, EDGE, W), F32), vmem((W, D), BF), vmem((3, W), F32)]
        + [vmem((R, mine, D), BF), vmem((TE, 3 * W), F32)],
        20,
    )((lengths,), (*gm_parts, *parts, *wo_pieces, wi_all, kernel, proj, mixin, normed1), ())
    o1, o3 = after((o1, o3), gm_parts[2])
    out_far = [swap(o3, "rows", 3), swap(o1, "rows", 1)]
    gn1_own, t1, t2, t3, norms = on_core(
        last_body, [shape((mine, D), F32)] + [shape((mine, D), BF)] * 3 + [shape((2, D), F32)]
    )((), (), (wi_here, gproj, xhat1, norm2_part))

    t1, t2, t3, sent3, sum2, out_far = join((t1, t2, t3, sent3, sum2, out_far))
    out_got += out_far
    (got3,) = near(sent3)
    gn1_got = [swap(t, "rows", k) for k, t in ((2, t2), (3, t3), (1, t1))]
    mine3, far3 = keep(keep3_body, (F, 4 * W), got3, normed_here, gproj, gm_all, mixin_here)
    far3 = swap(far3, "cols", 2)
    other2 = over(sum2)
    gn1_got, far3, other2 = join((gn1_got, far3, other2))
    sum3 = add_far(mine3, far3)
    other3 = over(sum3)

    norms = after(norms, sum3)
    sends = on_core(
        finish_body, [shape((mine + Q, F), BF)] * 4, [vmem((3, mine, D), BF), vmem((3, Q, D), BF)], 6
    )((), (*gn1_got, *out_got), (gn1_own, x_own, gains, grad_mid, mid_own, out_own, norms, kernel_part))
    got = exchange([sends[order.index(k)] for k in range(C)])
    input_grad, block_output, small = on_core(
        settle_body,
        [shape((S, F), F32), shape((S, F), BF), shape((EDGE, F), F32)],
        [vmem((C, mine + Q, F), BF)],
        4,
    )((), got, ())
    small = add_dp(small, over(small))

    sum1, sum2, other1, other2 = after((sum1, sum2, other1, other2), got[1])
    total1, total2 = add_dp(sum1, other1), add_dp(sum2, other2)
    total3 = add_dp(sum3, other3)
    down_grad = total1[:F].T
    gu_grad = jnp.stack([cat([total1[F:], total2[:half]], 0), total2[half:]], axis=1)
    in_grad = total3[:, : 3 * W].reshape(F, 3, W)
    out_grad = total3[:, 3 * W :].T
    return (
        block_output,
        input_grad,
        small[0],
        in_grad,
        small[2:5],
        out_grad,
        small[1],
        gu_grad,
        down_grad,
    )


def solution(mesh):
    tok = P(("dp", "rows"), "cols")
    feat = P("cols")
    wide = P("cols", None, "rows")
    tall = P("rows", "cols")
    taps = P(None, "rows")
    return jax.shard_map(
        local,
        mesh=mesh,
        in_specs=(tok, P("dp", None), feat, wide, taps, tall, feat, wide, tall, tok),
        out_specs=(tok, tok, feat, wide, taps, tall, feat, wide, tall),
        check_vma=False,
    )
```

```python
import functools

import jax
import jax.numpy as jnp
from jax import lax
from jax.experimental import pallas as pl
from jax.experimental.pallas import tpu as pltpu
from jax.sharding import PartitionSpec as P

EPS = 1e-06
BF = jnp.bfloat16
F32 = jnp.float32
EDGE = 8


def swap(value, axis, bit):
    size = lax.axis_size(axis)
    return lax.ppermute(value, axis, [(i, i ^ bit) for i in range(size)])


def dot(a, b):
    return jnp.dot(a, b, preferred_element_type=F32)


def dot_t(a, b):
    return lax.dot_general(a, b, (((1,), (1,)), ((), ())), preferred_element_type=F32)


def t_dot(a, b):
    return lax.dot_general(a, b, (((0,), (0,)), ((), ())), preferred_element_type=F32)


def low(v):
    return lax.reduce_precision(v, 8, 7).astype(BF)


def after(value, *first):
    return lax.optimization_barrier((value,) + first)[0]


def cat(parts, dim):
    return jnp.concatenate(parts, axis=dim)


def on_core(body, out, scratch=(), copies=0, limit=24):
    vmem, away = pl.BlockSpec(memory_space=pltpu.VMEM), pl.BlockSpec(memory_space=pltpu.HBM)

    def call(scalars, far, near):
        return pl.pallas_call(
            body,
            out_shape=[o[0] if isinstance(o, tuple) else o for o in out],
            in_specs=[pl.BlockSpec(memory_space=pltpu.SMEM)] * len(scalars)
            + [away] * len(far)
            + [vmem] * len(near),
            out_specs=[away if isinstance(o, tuple) else vmem for o in out],
            scratch_shapes=list(scratch) + ([pltpu.SemaphoreType.DMA((copies,))] if copies else []),
            compiler_params=pltpu.CompilerParams(vmem_limit_bytes=limit * 2**20),
            cost_estimate=pl.CostEstimate(flops=0, bytes_accessed=2**16, transcendentals=0),
        )(*scalars, *far, *near)

    return call


def pull(pairs, sems, first=0):
    started = []
    for i, (source, target) in enumerate(pairs):
        copy = pltpu.make_async_copy(source, target, sems.at[first + i])
        copy.start()
        started.append(copy)
    return started


def arrived(copies):
    for copy in copies:
        copy.wait()


def laid(target, pieces, dim):
    pairs, at = [], 0
    for piece in pieces:
        size = piece.shape[dim]
        place = target.at[pl.ds(at, size), :] if dim == 0 else target.at[:, pl.ds(at, size)]
        pairs.append((piece, place))
        at += size
    return pairs


def shape(dims, kind):
    return jax.ShapeDtypeStruct(dims, kind)


def stored(dims, kind):
    return (shape(dims, kind),)


def place_body(tokens, cotangent, gain1, gain2, p0, p1, p2, p3, edges, gains, sems):
    S = tokens.shape[0]
    Q = S // 4
    mine = Q + 2 * EDGE
    c = lax.axis_index("cols")
    outs = (p0, p1, p2, p3)
    soon = [(gain1, gains.at[0]), (gain2, gains.at[1])]
    later = []
    for k in range(4):
        start = pl.multiple_of((c ^ k) * Q, 16)
        early = pl.multiple_of(lax.rem(start + S - 16, S), 16)
        soon.append((tokens.at[pl.ds(early, 16), :], edges.at[k]))
        later.append((tokens.at[pl.ds(start, Q), :], outs[k].at[pl.ds(0, Q), :]))
        later.append((cotangent.at[pl.ds(start, Q), :], outs[k].at[pl.ds(mine, Q), :]))
    soon = pull(soon, sems)
    later = pull(later, sems, len(soon))
    arrived(soon)
    rows = lax.broadcasted_iota(jnp.int32, (EDGE, tokens.shape[1]), 0)
    values = jnp.zeros(rows.shape, F32)
    at = 0
    for i in range(2):
        left = gains[i]
        for _ in range(3):
            part = left.astype(BF).astype(F32)
            left = left - part
            values = jnp.where(rows == at, part, values)
            at += 1
    for k in range(4):
        edge = edges[k].astype(F32)[16 - EDGE :]
        outs[k][Q:mine, :] = jnp.concatenate([edge, values], axis=0).astype(BF)
    arrived(later)


def join_body(p0, p2, p1, p3, x_ref, dy_ref, g_ref, held, sems):
    F = p0.shape[1]
    Q = dy_ref.shape[0]
    copies = pull([(p, held.at[i]) for i, p in enumerate((p0, p2, p1, p3))], sems)
    for i, copy in enumerate(copies):
        copy.wait()
        cols = slice(i * F, (i + 1) * F)
        x_ref[:, cols] = held[i, : Q + 2 * EDGE]
        dy_ref[:, cols] = held[i, Q + 2 * EDGE :]
        t = held[i, Q : Q + 2 * EDGE].astype(F32)[EDGE:]
        g_ref[0:1, cols] = (t[0:1] + t[1:2]) + t[2:3]
        g_ref[1:2, cols] = (t[3:4] + t[4:5]) + t[5:6]


def chunk_taps(lengths, j, S, Q, W):
    z, c = lax.axis_index("rows"), lax.axis_index("cols")
    place = (z ^ j) * S + c * Q + lax.broadcasted_iota(jnp.int32, (Q, W), 0)
    end = jnp.int32(0)
    start = jnp.zeros_like(place)
    for i in range(lengths.shape[1]):
        end = end + lengths[0, i]
        start = jnp.where(place >= end, end, start)
    return [jnp.logical_and(place < end, place - start >= lag) for lag in range(3)]


def neighbour(j):
    z, c = lax.axis_index("rows"), lax.axis_index("cols")
    return jnp.where(c == 0, lax.rem((z ^ j) + 3, 4) ^ z, j)


def edge_products(proj_ref, edges, T, W):
    for j in range(4):
        lo = T + j * EDGE
        edges[j] = (proj_ref[lo : lo + EDGE, :W] * proj_ref[lo : lo + EDGE, 2 * W :]).astype(BF).astype(F32)


def tapped_lags(proj_ref, edges, taps, j, Q, W):
    lo = j * Q
    bv = (proj_ref[lo : lo + Q, :W] * proj_ref[lo : lo + Q, 2 * W :]).astype(BF).astype(F32)
    edge = edges[neighbour(j)]
    row = lax.broadcasted_iota(jnp.int32, (Q, W), 0)
    one = jnp.where(row == 0, edge[EDGE - 1 :], pltpu.roll(bv, 1, 0))
    two = pltpu.roll(bv, 2, 0)
    two = jnp.where(row == 0, edge[EDGE - 2 : EDGE - 1], jnp.where(row == 1, edge[EDGE - 1 :], two))
    return [jnp.where(tap, lagged, 0.0) for tap, lagged in zip(taps, (bv, one, two))]


def blocks_of(target, gathered, dim=0):
    c = lax.axis_index("cols")
    size = gathered.shape[0] // 4
    pairs = []
    for i, k in enumerate((0, 2, 1, 3)):
        width = gathered.shape[1]
        place = target.at[:, pl.ds(i * width, width)] if dim else target.at[pl.ds(i * size, size), :]
        start = pl.multiple_of((c ^ k) * size, 16)
        pairs.append((gathered.at[pl.ds(start, size), :], place))
    return pairs


def halved(target, pieces):
    if len(pieces) == 4:
        return laid(target, pieces, 0)
    y = lax.axis_index("dp")
    size = pieces[0].shape[0]
    half = size // 2
    pairs = []
    for h in range(2):
        own, first, second = pieces[3 * h : 3 * h + 3]
        base = 2 * size * h
        pairs.append((own, target.at[pl.ds(base, size), :]))
        for piece, at in ((first, y), (second, 1 - y)):
            start = pl.multiple_of(base + size + at * half, 16)
            pairs.append((piece, target.at[pl.ds(start, half), :]))
    return pairs


def split(refs, *counts):
    out = []
    for n in counts:
        out.append(refs[:n])
        refs = refs[n:]
    return out + [refs]


def mixer_body(lengths, r0, r1, r2, r3, kernel_in, w_in, gain, *refs):
    outs, (normed, proj, mixin, xs, w, edges, kernel, sems) = split(refs, 3)
    Q = xs.shape[1] - 2 * EDGE
    T = 4 * Q
    W = kernel.shape[1]
    tokens = pull([(r, xs.at[j]) for j, r in enumerate((r0, r1, r2, r3))], sems)
    tokens += pull([(kernel_in, kernel)], sems, 4)
    weights = pull(blocks_of(w, w_in), sems, 5)
    tail = []
    for j in range(4):
        tokens[j].wait()
        v = xs[j, : Q + EDGE, :].astype(F32)
        inv = lax.rsqrt(jnp.mean(v * v, axis=1, keepdims=True) + EPS)
        n = v * inv * gain[0:1, :]
        normed[j * Q : (j + 1) * Q, :] = n[:Q].astype(BF)
        tail.append(n[Q:])
    normed[T:, :] = jnp.concatenate(tail, axis=0).astype(BF)
    out = pull([(normed, outs[0])], sems, 9)
    arrived(weights + tokens[4:])
    for i in range(3):
        cols = slice(i * W, (i + 1) * W)
        proj[:, cols] = dot(normed[...], w[:, cols])
    out += pull([(proj, outs[1])], sems, 10)
    edge_products(proj, edges, T, W)
    for j in range(4):
        taps = chunk_taps(lengths, j, 4 * Q, Q, W)
        lags = tapped_lags(proj, edges, taps, j, Q, W)
        conv = kernel[0:1, :] * lags[0] + kernel[1:2, :] * lags[1] + kernel[2:3, :] * lags[2]
        rows = slice(j * Q, (j + 1) * Q)
        mixin[rows, :] = (proj[rows, W : 2 * W] * conv).astype(BF)
        out += pull([(mixin.at[pl.ds(j * Q, Q), :], outs[2].at[pl.ds(j * Q, Q), :])], sems, 11 + j)
    arrived(out)


def hidden_tiles(H):
    return [(h, min(256, H - h)) for h in range(0, H, 256)]


def forward_body(ng, *refs):
    rs, ms, wos, wgs, (gain,), rest = split(refs, 4, 4, 4, ng, 1)
    mid_own, normed, xhat, act, slope, silu_ref, wg, xs, mid, mix, wo, sems = rest
    T, W = ms[0].shape
    Q = T // 4
    H = act.shape[1]
    gain2 = gain[1:2, :]
    tokens = [(r.at[pl.ds(0, Q), :], xs.at[j]) for j, r in enumerate(rs)]
    blocks = [
        (ms[k].at[pl.ds((j ^ k) * Q, Q), :], mix.at[pl.ds(j * Q, Q), pl.ds(k * W, W)])
        for j in range(4)
        for k in range(4)
    ]
    outs = pull(laid(wo, wos, 1), sems)
    blocks = pull(blocks, sems, 4)
    tokens = pull(tokens, sems, 20)
    wide = pull(halved(wg, wgs), sems, 24)
    arrived(outs)
    for j in range(4):
        arrived(blocks[4 * j : 4 * j + 4])
        tokens[j].wait()
        rows = slice(j * Q, (j + 1) * Q)
        mid[rows, :] = xs[j].astype(F32) + dot(mix[rows, :], wo[...])
        v = mid[rows, :]
        inv = lax.rsqrt(jnp.mean(v * v, axis=1, keepdims=True) + EPS)
        xhat[rows, :] = v * inv
        normed[rows, :] = (v * inv * gain2).astype(BF)
    mid_own[...] = mid[:Q, :]
    arrived(wide)
    for h, size in hidden_tiles(H):
        cols, ups = slice(h, h + size), slice(H + h, H + h + size)
        gate = dot(normed[...], wg[:, cols])
        up = dot(normed[...], wg[:, ups])
        sig = 1.0 / (1.0 + jnp.exp(-gate))
        silu = gate * sig
        act[:, cols] = (silu * up).astype(BF)
        silu_ref[:, cols] = silu
        slope[:, cols] = up * sig * (1.0 + gate * (1.0 - sig))


def out_body(w_down, act, own, s1, s2, s3, wd, sems):
    Q, D = own.shape
    copies = pull(blocks_of(wd, w_down, 1), sems)
    for i, n in enumerate(range(0, D, D // 4)):
        cols = slice(n, n + D // 4)
        copies[i].wait()
        v = dot(act[...], wd[:, cols])
        own[:, cols] = v[:Q]
        for k, out in ((1, s1), (2, s2), (3, s3)):
            out[:, cols] = v[k * Q : (k + 1) * Q].astype(BF)


def turn_body(r0, r1, r2, r3, wd, slope, silu, gg, gu, dy_all, sems):
    H = gg.shape[1]
    arrived(pull(laid(dy_all, (r0, r1, r2, r3), 0), sems))
    for h, size in hidden_tiles(H):
        cols = slice(h, h + size)
        grad = dot_t(dy_all[...], wd[cols, :])
        gu[:, cols] = (grad * silu[:, cols]).astype(BF)
        gg[:, cols] = (grad * slope[:, cols]).astype(BF)


def sent_body(dy_all, act, normed, gg, gu, sent1, sent2):
    F = dy_all.shape[1] // 4
    H = act.shape[1]
    half = F // 2
    for i in range(2):
        at, to = (2 + i) * F, 3 * half * i
        for h, size in hidden_tiles(H):
            cols = slice(h, h + size)
            sent1[to : to + F, cols] = t_dot(dy_all[:, at : at + F], act[:, cols]).astype(BF)
            v = t_dot(normed[:, at : at + F], gg[:, cols]).astype(BF)
            sent1[to + F : to + 3 * half, cols] = v[:half]
            sent2[to : to + half, cols] = v[half:]
            sent2[to + half : to + 3 * half, cols] = t_dot(normed[:, at : at + F], gu[:, cols]).astype(BF)


def through_body(wg, gg, gu, xhat, own, s1, s2, s3, norm_part):
    Q, D = own.shape
    H = gg.shape[1]
    for n in range(0, D, D // 4):
        cols = slice(n, n + D // 4)
        v = dot_t(gg[...], wg[cols, :H]) + dot_t(gu[...], wg[cols, H:])
        norm_part[0:1, cols] = jnp.sum(v * xhat[:, cols], axis=0, keepdims=True)
        own[:, cols] = v[:Q]
        for k, out in ((1, s1), (2, s2), (3, s3)):
            out[:, cols] = v[k * Q : (k + 1) * Q].astype(BF)


def keep1_body(got_in, dy_all, act, normed, gg, mine, theirs, got, sems):
    rows = mine.shape[0]
    F = 2 * rows // 3
    half = F // 2
    H = act.shape[1]
    arrived(pull([(got_in, got)], sems))
    for i, out in enumerate((mine, theirs)):
        for h, size in hidden_tiles(H):
            cols = slice(h, h + size)
            v = t_dot(dy_all[:, i * F : (i + 1) * F], act[:, cols]) + got[i * rows : i * rows + F, cols].astype(F32)
            out[:F, cols] = v.astype(out.dtype)
            v = t_dot(normed[:, i * F : i * F + half], gg[:, cols]) + got[i * rows + F : (i + 1) * rows, cols].astype(F32)
            out[F:, cols] = v.astype(out.dtype)


def keep2_body(got_in, normed, gg, gu, mine, theirs, got, sems):
    rows = mine.shape[0]
    F = 2 * rows // 3
    half = F // 2
    H = gg.shape[1]
    arrived(pull([(got_in, got)], sems))
    for i, out in enumerate((mine, theirs)):
        for h, size in hidden_tiles(H):
            cols = slice(h, h + size)
            at = i * rows
            v = t_dot(normed[:, i * F + half : (i + 1) * F], gg[:, cols]) + got[at : at + half, cols].astype(F32)
            out[:half, cols] = v.astype(out.dtype)
            v = t_dot(normed[:, i * F : (i + 1) * F], gu[:, cols]) + got[at + half : at + rows, cols].astype(F32)
            out[half:, cols] = v.astype(out.dtype)


def keep3_body(got_in, normed, gproj, gm_all, mixin, mine, theirs, got, sems):
    F = mine.shape[0]
    W = mixin.shape[1]
    arrived(pull([(got_in, got)], sems))
    for i, out in enumerate((mine, theirs)):
        rows = slice(i * F, (i + 1) * F)
        for n in range(3):
            cols = slice(n * W, (n + 1) * W)
            out[:, cols] = (t_dot(normed[:, rows], gproj[:, cols]) + got[rows, cols].astype(F32)).astype(out.dtype)
        cols = slice(3 * W, 4 * W)
        out[:, cols] = (t_dot(gm_all[:, rows], mixin[...]) + got[rows, cols].astype(F32)).astype(out.dtype)


def back_body(lengths, *refs):
    gms, rs, wos, (w_in, kernel_in, proj_in, mixin_in, normed_in), rest = split(refs, 4, 4, 4, 5)
    gproj, gm_all, xhat, sent, kernel_part, mixin, normed, wi, edges, back, wo, kernel, xs, proj, sems = rest
    Q = gms[0].shape[0]
    T = 4 * Q
    W = kernel.shape[1]
    DH = wo.shape[1] // 2
    row = lax.broadcasted_iota(jnp.int32, (Q, W), 0)
    soon = pull([(proj_in, proj)], sems)
    tokens = pull([(r, xs.at[j]) for j, r in enumerate(rs)], sems, 1)
    copies = pull(
        laid(gm_all, gms, 0)
        + laid(wo, [w.at[pl.ds(0, W), :] for w in wos], 1)
        + [(kernel_in, kernel), (mixin_in, mixin), (normed_in, normed)],
        sems,
        5,
    )
    weights = pull(blocks_of(wi, w_in), sems, 16)
    arrived(soon)
    edge_products(proj, edges, T, W)
    back[...] = jnp.zeros(back.shape, F32)
    arrived(copies)
    sums = [jnp.zeros((1, W), F32)] * 3
    tail = []
    for j in range(4):
        rows = slice(j * Q, (j + 1) * Q)
        grad_mix = dot_t(gm_all[rows, :], wo[...])
        taps = chunk_taps(lengths, j, 4 * Q, Q, W)
        lags = tapped_lags(proj, edges, taps, j, Q, W)
        conv = kernel[0:1, :] * lags[0] + kernel[1:2, :] * lags[1] + kernel[2:3, :] * lags[2]
        grad_conv = (grad_mix * proj[rows, W : 2 * W]).astype(BF).astype(F32)
        sums = [s + jnp.sum(grad_conv * lag, axis=0, keepdims=True) for s, lag in zip(sums, lags)]
        m0, m1, m2 = [jnp.where(tap, grad_conv, 0.0) for tap in taps]
        m1 = kernel[1:2, :] * m1
        m2 = kernel[2:3, :] * m2
        grad_bv = kernel[0:1, :] * m0
        grad_bv = grad_bv + jnp.where(row < Q - 1, pltpu.roll(m1, Q - 1, 0), 0.0)
        grad_bv = grad_bv + jnp.where(row < Q - 2, pltpu.roll(m2, Q - 2, 0), 0.0)
        head = lax.broadcasted_iota(jnp.int32, (EDGE, W), 0)
        last = jnp.where(head == EDGE - 1, m1[0:1] + m2[1:2], 0.0)
        back[neighbour(j)] = jnp.where(head == EDGE - 2, m2[0:1], last)
        gproj[rows, :W] = (grad_bv * proj[rows, 2 * W :]).astype(BF)
        gproj[rows, W : 2 * W] = (grad_mix * conv).astype(BF)
        gproj[rows, 2 * W :] = (grad_bv * proj[rows, :W]).astype(BF)
    for i in range(3):
        kernel_part[i : i + 1, :] = sums[i]
    for j in range(4):
        lo = T + j * EDGE
        tail.append(
            jnp.concatenate(
                [back[j] * proj[lo : lo + EDGE, 2 * W :], jnp.zeros((EDGE, W), F32), back[j] * proj[lo : lo + EDGE, :W]],
                axis=1,
            )
        )
    gproj[T:, :] = jnp.concatenate(tail, axis=0).astype(BF)
    for i in range(3):
        cols = slice(i * W, (i + 1) * W)
        sent[:, cols] = t_dot(normed[:, DH:], gproj[:, cols]).astype(BF)
    sent[:, 3 * W :] = t_dot(gm_all[:, DH:], mixin[...]).astype(BF)
    for j in range(4):
        tokens[j].wait()
        v = xs[j, : Q + EDGE, :].astype(F32)
        v = v * lax.rsqrt(jnp.mean(v * v, axis=1, keepdims=True) + EPS)
        xhat[j * Q : (j + 1) * Q, :] = v[:Q]
        xhat[T + j * EDGE : T + (j + 1) * EDGE, :] = v[Q:]
    arrived(weights)


def last_body(w, gproj, xhat, norm2, own, s1, s2, s3, norms):
    D = own.shape[1]
    Q = own.shape[0] - 2 * EDGE
    T = 4 * Q
    head = lax.broadcasted_iota(jnp.int32, (EDGE, D // 4), 0)
    for n in range(0, D, D // 4):
        cols = slice(n, n + D // 4)
        v = dot_t(gproj[...], w[cols, :])
        one = jnp.sum(v * xhat[:, cols], axis=0, keepdims=True).astype(BF).astype(F32)
        two = norm2[:, cols].astype(BF).astype(F32)
        norms[0:1, cols] = one
        norms[1:2, cols] = two
        more = jnp.where(head == 0, one, jnp.where(head == 1, two, 0.0))
        for k, out in enumerate((own, s1, s2, s3)):
            out[:Q, cols] = v[k * Q : (k + 1) * Q].astype(out.dtype)
            edge = v[T + k * EDGE : T + (k + 1) * EDGE]
            out[Q:, cols] = jnp.concatenate([edge, more], axis=0).astype(out.dtype)


def finish_body(g2, g3, g1, o2, o3, o1, own, x_own, gain, grad_mid, mid_own, out_own, norms, kernel_part, p0, p2, p1, p3, got, got_out, sems):
    Q, D = out_own.shape
    E = Q + EDGE
    F = D // 4
    copies = pull([(g, got.at[i]) for i, g in enumerate((g2, g3, g1))], sems)
    outer = pull([(o, got_out.at[i]) for i, o in enumerate((o2, o3, o1))], sems, 3)
    x = x_own[...].astype(F32)[:E]
    inv = lax.rsqrt(jnp.mean(x * x, axis=1, keepdims=True) + EPS)
    arrived(copies)
    two, three, one = [got[i].astype(F32) for i in range(3)]
    total = (norms[...] + one[E : E + 2]) + (two[E : E + 2] + three[E : E + 2])
    grad = own[:E, :] + two[:E] + three[:E] + one[:E]
    scaled = grad * gain[0:1, :]
    inner = jnp.mean(scaled * x, axis=1, keepdims=True)
    res = inv * scaled - x * (inv * inv * inv * inner)
    arrived(outer)
    out = mid_own[...] + out_own[...]
    for i in range(3):
        out = out + got_out[i].astype(F32)
    main = res[:Q] + grad_mid[...]
    small = jnp.concatenate([total, jnp.zeros((EDGE - 2, D), F32)], axis=0)
    row = lax.broadcasted_iota(jnp.int32, (EDGE, F), 0)
    for i, piece in enumerate((p0, p2, p1, p3)):
        cols = slice(i * F, (i + 1) * F)
        sums = small[:, cols]
        for n in range(3):
            sums = jnp.where(row == 2 + n, kernel_part[n : n + 1, :], sums)
        edge = jnp.concatenate([res[Q:, cols], sums], axis=0)
        piece[:Q, :] = main[:, cols].astype(BF)
        piece[Q : Q + 2 * EDGE, :] = edge.astype(BF)
        piece[Q + 2 * EDGE :, :] = out[:, cols].astype(BF)


def settle_body(p0, p1, p2, p3, grad_ref, out_ref, small, held, sems):
    S = grad_ref.shape[0]
    Q = S // 4
    c = lax.axis_index("cols")
    copies = pull([(p, held.at[k]) for k, p in enumerate((p0, p1, p2, p3))], sems)
    arrived(copies)
    for k in range(4):
        start = pl.multiple_of((c ^ k) * Q, 16)
        grad_ref[pl.ds(start, Q), :] = held[k, :Q].astype(F32)
        out_ref[pl.ds(start, Q), :] = held[k, Q + 2 * EDGE :]
    for k in range(4):
        before = pl.multiple_of(lax.rem((c ^ k) * Q + S - EDGE, S), 8)
        grad_ref[pl.ds(before, EDGE), :] += held[k, Q : Q + 2 * EDGE].astype(F32)[:EDGE]
    s0, s1, s2, s3 = [held[k, Q : Q + 2 * EDGE].astype(F32)[EDGE:] for k in range(4)]
    small[...] = (s0 + s1) + (s2 + s3)


def total_body(twin, other_in, mine, in_ref, out_ref, other, sems):
    W = in_ref.shape[2]
    arrived(pull([(other_in, other)], sems))
    for n in range(4):
        cols = slice(n * W, (n + 1) * W)
        v = mine[:, cols].astype(F32)
        if twin:
            v = v + other[:, cols].astype(F32)
        if n < 3:
            in_ref[:, n, :] = v
        else:
            out_ref[...] = v.T


def local(tokens, lengths, gain1, w_in, kernel, w_out, gain2, w_gu, w_down, cotangent):
    S, F = tokens.shape
    R, C = lax.axis_size("rows"), lax.axis_size("cols")
    assert R == 4 and C == 4
    y = lax.axis_index("dp")
    twin = lax.axis_size("dp") == 2
    Q = S // C
    E = Q + EDGE
    T = R * Q
    TE = R * E
    W = w_out.shape[0]
    H = w_down.shape[0]
    D = C * F
    DH = 2 * F
    half = F // 2

    order = (0, 2, 1, 3)

    def exchange(pieces):
        return [pieces[0]] + [swap(pieces[k], "cols", k) for k in (1, 2, 3)]

    def gather_rows(a):
        far_two = swap(a, "rows", 2)
        far_three = swap(a, "rows", 3)
        return [a, swap(a, "rows", 1), far_two, far_three]

    def over(v):
        return swap(v, "dp", 1)

    def near(*vs):
        return [swap(v, "cols", 1) for v in vs]

    join = lax.optimization_barrier
    vmem = pltpu.VMEM
    mine = E + EDGE

    placed = on_core(
        place_body, [shape((mine + Q, F), BF)] * 4, [vmem((R, 16, F), BF), vmem((2, 1, F), F32)], 14, 60
    )((), (tokens, cotangent, gain1.reshape(1, F), gain2.reshape(1, F)), ())
    pieces = exchange(placed)
    wi_all = lax.all_gather(w_in.reshape(F, 3 * W), "cols", tiled=True)
    wo = after(w_out, placed[0])
    if twin:
        wo = jnp.where(y == 0, wo[:, : F // 2], wo[:, F // 2 :])
    wg = after(w_gu, placed[0]).reshape(F, 2 * H)
    pieces, wo_parts, wg = join((pieces, gather_rows(wo), wg))
    x_own, dy_own, gains = on_core(
        join_body,
        [shape((mine, D), BF), shape((Q, D), BF), shape((2, D), F32)],
        [vmem((C, mine + Q, F), BF)],
        4,
    )((), [pieces[k] for k in order], ())

    parts = gather_rows(x_own)
    wo = cat(wo_parts, 0)
    if twin:
        wo_other = swap(wo, "dp", 1)
        wo = cat([jnp.where(y == 0, wo, wo_other), jnp.where(y == 0, wo_other, wo)], 1)
    wg_half = wg
    if twin:
        wg_half = jnp.where(y == 0, wg[: F // 2], wg[F // 2 :])
    wg_far = swap(after(wg_half, x_own), "cols", 2)
    wd_all = lax.all_gather(after(w_down, x_own), "cols", tiled=True)
    parts = join(parts)
    normed1, proj, mixin = on_core(
        mixer_body,
        [stored((TE, D), BF), stored((TE, 3 * W), F32), stored((T, W), BF)],
        [vmem((TE, D), BF), vmem((TE, 3 * W), F32), vmem((T, W), BF), vmem((R, mine, D), BF), vmem((D, 3 * W), BF)]
        + [vmem((R, EDGE, W), F32), vmem((3, W), F32)],
        15,
        60,
    )((lengths,), (*parts, kernel, wi_all), (gains,))

    mixin, wg_far, wo = join((mixin, wg_far, wo))
    mix_parts = gather_rows(mixin)
    wo_far = swap(wo, "cols", 2)
    wg_fars = [wg_far, swap(wg_far, "dp", 1)] if twin else [wg_far]
    mix_parts, wo_far, wo, wg_fars, wd_all, wg = join((mix_parts, wo_far, wo, wg_fars, wd_all, wg))
    wg_pieces = [wg] + wg_fars + near(wg, *wg_fars)
    wo_pieces = [wo, wo_far] + near(wo, wo_far)

    dy_parts = gather_rows(after(dy_own, mix_parts[1]))
    mid_own, normed2, xhat2, act, slope, silu, wg_here = on_core(
        functools.partial(forward_body, len(wg_pieces)),
        [shape((Q, D), F32), shape((T, D), BF), shape((T, D), F32), shape((T, H), BF), shape((T, H), F32), shape((T, H), F32)]
        + [shape((D, 2 * H), BF)],
        [vmem((R, Q, D), BF), vmem((T, D), F32), vmem((T, D), BF), vmem((D, D), BF)],
        24 + len(wg_pieces),
    )((), (*parts, *mix_parts, *wo_pieces, *wg_pieces), (gains,))
    out_own, o1, o2, o3, wd_here = on_core(
        out_body, [shape((Q, D), F32)] + [shape((Q, D), BF)] * 3 + [shape((H, D), BF)], (), 4
    )((), (wd_all,), (act,))
    dy_parts, o1, o2, o3, wd_here = join((dy_parts, o1, o2, o3, wd_here))

    grad_gate, grad_up, dy_all = on_core(
        turn_body, [shape((T, H), BF)] * 2 + [shape((T, D), BF)], (), 4
    )((), dy_parts, (wd_here, slope, silu))
    gn2_own, t1, t2, t3, norm2_part = on_core(
        through_body, [shape((Q, D), F32)] + [shape((Q, D), BF)] * 3 + [shape((1, D), F32)]
    )((), (), (wg_here, grad_gate, grad_up, xhat2))

    def keep(body, size, got, *arrays):
        return on_core(body, [shape(size, F32), shape(size, BF)], [vmem(got.shape, BF)], 1)((), (got,), arrays)

    def add_far(mine, got):
        return low(mine + got.astype(F32))

    def add_dp(mine, other):
        if twin:
            return mine.astype(F32) + other.astype(F32)
        return lax.psum(mine.astype(F32), "dp")

    def over(v):
        return swap(v, "dp", 1) if twin else v

    third = 3 * half
    t1, t2, t3, grad_gate, grad_up = join((t1, t2, t3, grad_gate, grad_up))
    gn2_got = [swap(t, "rows", k) for k, t in ((2, t2), (3, t3), (1, t1))]
    sent1, sent2 = on_core(sent_body, [shape((third * 2, H), BF)] * 2)(
        (), (), (dy_all, act, normed2, grad_gate, grad_up)
    )
    got1, got2 = near(sent1, sent2)
    mine1, far1 = keep(keep1_body, (third, H), got1, dy_all, act, normed2, grad_gate)
    mine2, far2 = keep(keep2_body, (third, H), got2, normed2, grad_gate, grad_up)
    gn2_got, far1, far2 = join((gn2_got, far1, far2))
    for g in gn2_got:
        gn2_own = gn2_own + g.astype(F32)
    inv2_own = lax.rsqrt(jnp.mean(mid_own * mid_own, axis=1, keepdims=True) + EPS)
    scaled = gn2_own * gains[1:2]
    inner = jnp.mean(scaled * mid_own, axis=1, keepdims=True)
    grad_mid = dy_own.astype(F32) + inv2_own * scaled - mid_own * (inv2_own**3 * inner)

    gm_low, far1 = join((grad_mid.astype(BF), far1))
    gm_parts = gather_rows(gm_low)
    far1 = swap(far1, "cols", 2)
    gm_parts, far1, far2 = join((gm_parts, far1, far2))

    sum1 = add_far(mine1, far1)
    far2 = swap(far2, "cols", 2)
    other1 = over(sum1)
    out_got = [swap(after(o, gm_parts[2]), "rows", k) for k, o in ((2, o2), (3, o3), (1, o1))]
    gproj, gm_all, xhat1, sent3, kernel_part, mixin_here, normed_here, wi_here = on_core(
        back_body,
        [shape((TE, 3 * W), BF), shape((T, D), BF), shape((TE, D), F32), shape((DH, 4 * W), BF), shape((3, W), F32)]
        + [shape((T, W), BF), shape((TE, D), BF), shape((D, 3 * W), BF)],
        [vmem((R, EDGE, W), F32), vmem((R, EDGE, W), F32), vmem((W, D), BF), vmem((3, W), F32)]
        + [vmem((R, mine, D), BF), vmem((TE, 3 * W), F32)],
        20,
    )((lengths,), (*gm_parts, *parts, *wo_pieces, wi_all, kernel, proj, mixin, normed1), ())
    gn1_own, t1, t2, t3, norms = on_core(
        last_body, [shape((mine, D), F32)] + [shape((mine, D), BF)] * 3 + [shape((2, D), F32)]
    )((), (), (wi_here, gproj, xhat1, norm2_part))

    t1, t2, t3, sent3, far2, other1, out_got = join((t1, t2, t3, sent3, far2, other1, out_got))
    sum2 = add_far(mine2, far2)
    (got3,) = near(sent3)
    gn1_got = [swap(t, "rows", k) for k, t in ((2, t2), (3, t3), (1, t1))]
    mine3, far3 = keep(keep3_body, (F, 4 * W), got3, normed_here, gproj, gm_all, mixin_here)
    far3 = swap(far3, "cols", 2)
    other2 = over(sum2)
    gn1_got, far3, other2 = join((gn1_got, far3, other2))
    sum3 = add_far(mine3, far3)
    other3 = over(sum3)

    norms = after(norms, sum3)
    sends = on_core(
        finish_body, [shape((mine + Q, F), BF)] * 4, [vmem((3, mine, D), BF), vmem((3, Q, D), BF)], 6
    )((), (*gn1_got, *out_got), (gn1_own, x_own, gains, grad_mid, mid_own, out_own, norms, kernel_part))
    got = exchange([sends[order.index(k)] for k in range(C)])
    input_grad, block_output, small = on_core(
        settle_body,
        [shape((S, F), F32), shape((S, F), BF), shape((EDGE, F), F32)],
        [vmem((C, mine + Q, F), BF)],
        4,
    )((), got, ())
    small = add_dp(small, over(small))

    sum1, sum2, other1, other2 = after((sum1, sum2, other1, other2), got[1])
    total1, total2 = add_dp(sum1, other1), add_dp(sum2, other2)
    down_grad = total1[:F].T
    gu_grad = jnp.stack([cat([total1[F:], total2[:half]], 0), total2[half:]], axis=1)
    if not twin:
        sum3 = lax.psum(sum3.astype(F32), "dp")
        other3 = sum3
    in_grad, out_grad = on_core(
        functools.partial(total_body, twin),
        [shape((F, 3, W), F32), shape((W, F), F32)],
        [vmem(other3.shape, other3.dtype)],
        1,
    )((), (other3,), (sum3,))
    return (
        block_output,
        input_grad,
        small[0],
        in_grad,
        small[2:5],
        out_grad,
        small[1],
        gu_grad,
        down_grad,
    )


def solution(mesh):
    tok = P(("dp", "rows"), "cols")
    feat = P("cols")
    wide = P("cols", None, "rows")
    tall = P("rows", "cols")
    taps = P(None, "rows")
    return jax.shard_map(
        local,
        mesh=mesh,
        in_specs=(tok, P("dp", None), feat, wide, taps, tall, feat, wide, tall, tok),
        out_specs=(tok, tok, feat, wide, taps, tall, feat, wide, tall),
        check_vma=False,
    )
```

```python
import functools

import jax
import jax.numpy as jnp
from jax import lax
from jax.experimental import pallas as pl
from jax.experimental.pallas import tpu as pltpu
from jax.sharding import PartitionSpec as P

EPS = 1e-06
BF = jnp.bfloat16
F32 = jnp.float32
EDGE = 8


def swap(value, axis, bit):
    size = lax.axis_size(axis)
    return lax.ppermute(value, axis, [(i, i ^ bit) for i in range(size)])


def dot(a, b):
    return jnp.dot(a, b, preferred_element_type=F32)


def dot_t(a, b):
    return lax.dot_general(a, b, (((1,), (1,)), ((), ())), preferred_element_type=F32)


def t_dot(a, b):
    return lax.dot_general(a, b, (((0,), (0,)), ((), ())), preferred_element_type=F32)


def low(v):
    return lax.reduce_precision(v, 8, 7).astype(BF)


def after(value, *first):
    return lax.optimization_barrier((value,) + first)[0]


def cat(parts, dim):
    return jnp.concatenate(parts, axis=dim)


def on_core(body, out, scratch=(), copies=0, limit=24):
    vmem, away = pl.BlockSpec(memory_space=pltpu.VMEM), pl.BlockSpec(memory_space=pltpu.HBM)

    def call(scalars, far, near):
        return pl.pallas_call(
            body,
            out_shape=[o[0] if isinstance(o, tuple) else o for o in out],
            in_specs=[pl.BlockSpec(memory_space=pltpu.SMEM)] * len(scalars)
            + [away] * len(far)
            + [vmem] * len(near),
            out_specs=[away if isinstance(o, tuple) else vmem for o in out],
            scratch_shapes=list(scratch) + ([pltpu.SemaphoreType.DMA((copies,))] if copies else []),
            compiler_params=pltpu.CompilerParams(vmem_limit_bytes=limit * 2**20),
            cost_estimate=pl.CostEstimate(flops=0, bytes_accessed=2**16, transcendentals=0),
        )(*scalars, *far, *near)

    return call


def pull(pairs, sems, first=0):
    started = []
    for i, (source, target) in enumerate(pairs):
        copy = pltpu.make_async_copy(source, target, sems.at[first + i])
        copy.start()
        started.append(copy)
    return started


def arrived(copies):
    for copy in copies:
        copy.wait()


def laid(target, pieces, dim):
    pairs, at = [], 0
    for piece in pieces:
        size = piece.shape[dim]
        place = target.at[pl.ds(at, size), :] if dim == 0 else target.at[:, pl.ds(at, size)]
        pairs.append((piece, place))
        at += size
    return pairs


def shape(dims, kind):
    return jax.ShapeDtypeStruct(dims, kind)


def stored(dims, kind):
    return (shape(dims, kind),)


def place_body(tokens, cotangent, gain1, gain2, p0, p1, p2, p3, edges, gains, sems):
    S = tokens.shape[0]
    Q = S // 4
    mine = Q + 2 * EDGE
    c = lax.axis_index("cols")
    outs = (p0, p1, p2, p3)
    soon = [(gain1, gains.at[0]), (gain2, gains.at[1])]
    later = []
    for k in range(4):
        start = pl.multiple_of((c ^ k) * Q, 16)
        early = pl.multiple_of(lax.rem(start + S - 16, S), 16)
        soon.append((tokens.at[pl.ds(early, 16), :], edges.at[k]))
        later.append((tokens.at[pl.ds(start, Q), :], outs[k].at[pl.ds(0, Q), :]))
        later.append((cotangent.at[pl.ds(start, Q), :], outs[k].at[pl.ds(mine, Q), :]))
    soon = pull(soon, sems)
    later = pull(later, sems, len(soon))
    arrived(soon)
    rows = lax.broadcasted_iota(jnp.int32, (EDGE, tokens.shape[1]), 0)
    values = jnp.zeros(rows.shape, F32)
    at = 0
    for i in range(2):
        left = gains[i]
        for _ in range(3):
            part = left.astype(BF).astype(F32)
            left = left - part
            values = jnp.where(rows == at, part, values)
            at += 1
    for k in range(4):
        edge = edges[k].astype(F32)[16 - EDGE :]
        outs[k][Q:mine, :] = jnp.concatenate([edge, values], axis=0).astype(BF)
    arrived(later)


def join_body(p0, p2, p1, p3, x_ref, dy_ref, g_ref, held, sems):
    F = p0.shape[1]
    Q = dy_ref.shape[0]
    copies = pull([(p, held.at[i]) for i, p in enumerate((p0, p2, p1, p3))], sems)
    for i, copy in enumerate(copies):
        copy.wait()
        cols = slice(i * F, (i + 1) * F)
        x_ref[:, cols] = held[i, : Q + 2 * EDGE]
        dy_ref[:, cols] = held[i, Q + 2 * EDGE :]
        t = held[i, Q : Q + 2 * EDGE].astype(F32)[EDGE:]
        g_ref[0:1, cols] = (t[0:1] + t[1:2]) + t[2:3]
        g_ref[1:2, cols] = (t[3:4] + t[4:5]) + t[5:6]


def chunk_taps(lengths, j, S, Q, W):
    z, c = lax.axis_index("rows"), lax.axis_index("cols")
    place = (z ^ j) * S + c * Q + lax.broadcasted_iota(jnp.int32, (Q, W), 0)
    end = jnp.int32(0)
    start = jnp.zeros_like(place)
    for i in range(lengths.shape[1]):
        end = end + lengths[0, i]
        start = jnp.where(place >= end, end, start)
    return [jnp.logical_and(place < end, place - start >= lag) for lag in range(3)]


def neighbour(j):
    z, c = lax.axis_index("rows"), lax.axis_index("cols")
    return jnp.where(c == 0, lax.rem((z ^ j) + 3, 4) ^ z, j)


def edge_products(proj_ref, edges, T, W):
    for j in range(4):
        lo = T + j * EDGE
        edges[j] = (proj_ref[lo : lo + EDGE, :W] * proj_ref[lo : lo + EDGE, 2 * W :]).astype(BF).astype(F32)


def tapped_lags(proj_ref, edges, taps, j, Q, W):
    lo = j * Q
    bv = (proj_ref[lo : lo + Q, :W] * proj_ref[lo : lo + Q, 2 * W :]).astype(BF).astype(F32)
    edge = edges[neighbour(j)]
    row = lax.broadcasted_iota(jnp.int32, (Q, W), 0)
    one = jnp.where(row == 0, edge[EDGE - 1 :], pltpu.roll(bv, 1, 0))
    two = pltpu.roll(bv, 2, 0)
    two = jnp.where(row == 0, edge[EDGE - 2 : EDGE - 1], jnp.where(row == 1, edge[EDGE - 1 :], two))
    return [jnp.where(tap, lagged, 0.0) for tap, lagged in zip(taps, (bv, one, two))]


def blocks_of(target, gathered, dim=0):
    c = lax.axis_index("cols")
    size = gathered.shape[0] // 4
    pairs = []
    for i, k in enumerate((0, 2, 1, 3)):
        width = gathered.shape[1]
        place = target.at[:, pl.ds(i * width, width)] if dim else target.at[pl.ds(i * size, size), :]
        start = pl.multiple_of((c ^ k) * size, 16)
        pairs.append((gathered.at[pl.ds(start, size), :], place))
    return pairs


def halved(target, pieces):
    if len(pieces) == 4:
        return laid(target, pieces, 0)
    y = lax.axis_index("dp")
    size = pieces[0].shape[0]
    half = size // 2
    pairs = []
    for h in range(2):
        own, first, second = pieces[3 * h : 3 * h + 3]
        base = 2 * size * h
        pairs.append((own, target.at[pl.ds(base, size), :]))
        for piece, at in ((first, y), (second, 1 - y)):
            start = pl.multiple_of(base + size + at * half, 16)
            pairs.append((piece, target.at[pl.ds(start, half), :]))
    return pairs


def split(refs, *counts):
    out = []
    for n in counts:
        out.append(refs[:n])
        refs = refs[n:]
    return out + [refs]


def mixer_body(lengths, r0, r1, r2, r3, kernel_in, w_in, gain, *refs):
    outs, (normed, proj, mixin, xs, w, edges, kernel, sems) = split(refs, 3)
    Q = xs.shape[1] - 2 * EDGE
    T = 4 * Q
    W = kernel.shape[1]
    tokens = pull([(r, xs.at[j]) for j, r in enumerate((r0, r1, r2, r3))], sems)
    tokens += pull([(kernel_in, kernel)], sems, 4)
    weights = pull(blocks_of(w, w_in), sems, 5)
    tail = []
    for j in range(4):
        tokens[j].wait()
        v = xs[j, : Q + EDGE, :].astype(F32)
        inv = lax.rsqrt(jnp.mean(v * v, axis=1, keepdims=True) + EPS)
        n = v * inv * gain[0:1, :]
        normed[j * Q : (j + 1) * Q, :] = n[:Q].astype(BF)
        tail.append(n[Q:])
    normed[T:, :] = jnp.concatenate(tail, axis=0).astype(BF)
    out = pull([(normed, outs[0])], sems, 9)
    arrived(weights + tokens[4:])
    for i in range(3):
        cols = slice(i * W, (i + 1) * W)
        proj[:, cols] = dot(normed[...], w[:, cols])
    out += pull([(proj, outs[1])], sems, 10)
    edge_products(proj, edges, T, W)
    for j in range(4):
        taps = chunk_taps(lengths, j, 4 * Q, Q, W)
        lags = tapped_lags(proj, edges, taps, j, Q, W)
        conv = kernel[0:1, :] * lags[0] + kernel[1:2, :] * lags[1] + kernel[2:3, :] * lags[2]
        rows = slice(j * Q, (j + 1) * Q)
        mixin[rows, :] = (proj[rows, W : 2 * W] * conv).astype(BF)
        out += pull([(mixin.at[pl.ds(j * Q, Q), :], outs[2].at[pl.ds(j * Q, Q), :])], sems, 11 + j)
    arrived(out)


def hidden_tiles(H):
    return [(h, min(256, H - h)) for h in range(0, H, 256)]


def forward_body(ng, *refs):
    rs, ms, wos, wgs, (gain,), rest = split(refs, 4, 4, 4, ng, 1)
    mid_own, normed, xhat, act, slope, silu_ref, wg, xs, mid, mix, wo, sems = rest
    T, W = ms[0].shape
    Q = T // 4
    H = act.shape[1]
    gain2 = gain[1:2, :]
    tokens = [(r.at[pl.ds(0, Q), :], xs.at[j]) for j, r in enumerate(rs)]
    blocks = [
        (ms[k].at[pl.ds((j ^ k) * Q, Q), :], mix.at[pl.ds(j * Q, Q), pl.ds(k * W, W)])
        for j in range(4)
        for k in range(4)
    ]
    outs = pull(laid(wo, wos, 1), sems)
    blocks = pull(blocks, sems, 4)
    tokens = pull(tokens, sems, 20)
    wide = pull(halved(wg, wgs), sems, 24)
    arrived(outs)
    for j in range(4):
        arrived(blocks[4 * j : 4 * j + 4])
        tokens[j].wait()
        rows = slice(j * Q, (j + 1) * Q)
        mid[rows, :] = xs[j].astype(F32) + dot(mix[rows, :], wo[...])
        v = mid[rows, :]
        inv = lax.rsqrt(jnp.mean(v * v, axis=1, keepdims=True) + EPS)
        xhat[rows, :] = v * inv
        normed[rows, :] = (v * inv * gain2).astype(BF)
    mid_own[...] = mid[:Q, :]
    arrived(wide)
    for h, size in hidden_tiles(H):
        cols, ups = slice(h, h + size), slice(H + h, H + h + size)
        gate = dot(normed[...], wg[:, cols])
        up = dot(normed[...], wg[:, ups])
        sig = 1.0 / (1.0 + jnp.exp(-gate))
        silu = gate * sig
        act[:, cols] = (silu * up).astype(BF)
        silu_ref[:, cols] = silu
        slope[:, cols] = up * sig * (1.0 + gate * (1.0 - sig))


def out_body(w_down, act, own, s1, s2, s3, wd, sems):
    Q, D = own.shape
    copies = pull(blocks_of(wd, w_down, 1), sems)
    for i, n in enumerate(range(0, D, D // 4)):
        cols = slice(n, n + D // 4)
        copies[i].wait()
        v = dot(act[...], wd[:, cols])
        own[:, cols] = v[:Q]
        for k, out in ((1, s1), (2, s2), (3, s3)):
            out[:, cols] = v[k * Q : (k + 1) * Q].astype(BF)


def turn_body(r0, r1, r2, r3, wd, slope, silu, gg, gu, dy_all, sems):
    H = gg.shape[1]
    arrived(pull(laid(dy_all, (r0, r1, r2, r3), 0), sems))
    for h, size in hidden_tiles(H):
        cols = slice(h, h + size)
        grad = dot_t(dy_all[...], wd[cols, :])
        gu[:, cols] = (grad * silu[:, cols]).astype(BF)
        gg[:, cols] = (grad * slope[:, cols]).astype(BF)


def sent_body(dy_all, act, normed, gg, gu, sent1, sent2):
    F = dy_all.shape[1] // 4
    H = act.shape[1]
    half = F // 2
    for i in range(2):
        at, to = (2 + i) * F, 3 * half * i
        for h, size in hidden_tiles(H):
            cols = slice(h, h + size)
            sent1[to : to + F, cols] = t_dot(dy_all[:, at : at + F], act[:, cols]).astype(BF)
            v = t_dot(normed[:, at : at + F], gg[:, cols]).astype(BF)
            sent1[to + F : to + 3 * half, cols] = v[:half]
            sent2[to : to + half, cols] = v[half:]
            sent2[to + half : to + 3 * half, cols] = t_dot(normed[:, at : at + F], gu[:, cols]).astype(BF)


def through_body(wg, gg, gu, xhat, own, s1, s2, s3, norm_part):
    Q, D = own.shape
    H = gg.shape[1]
    for n in range(0, D, D // 4):
        cols = slice(n, n + D // 4)
        v = dot_t(gg[...], wg[cols, :H]) + dot_t(gu[...], wg[cols, H:])
        norm_part[0:1, cols] = jnp.sum(v * xhat[:, cols], axis=0, keepdims=True)
        own[:, cols] = v[:Q]
        for k, out in ((1, s1), (2, s2), (3, s3)):
            out[:, cols] = v[k * Q : (k + 1) * Q].astype(BF)


def keep1_body(got_in, dy_all, act, normed, gg, mine, theirs, got, sems):
    rows = mine.shape[0]
    F = 2 * rows // 3
    half = F // 2
    H = act.shape[1]
    arrived(pull([(got_in, got)], sems))
    for i, out in enumerate((mine, theirs)):
        for h, size in hidden_tiles(H):
            cols = slice(h, h + size)
            v = t_dot(dy_all[:, i * F : (i + 1) * F], act[:, cols]) + got[i * rows : i * rows + F, cols].astype(F32)
            out[:F, cols] = v.astype(out.dtype)
            v = t_dot(normed[:, i * F : i * F + half], gg[:, cols]) + got[i * rows + F : (i + 1) * rows, cols].astype(F32)
            out[F:, cols] = v.astype(out.dtype)


def keep2_body(got_in, normed, gg, gu, mine, theirs, got, sems):
    rows = mine.shape[0]
    F = 2 * rows // 3
    half = F // 2
    H = gg.shape[1]
    arrived(pull([(got_in, got)], sems))
    for i, out in enumerate((mine, theirs)):
        for h, size in hidden_tiles(H):
            cols = slice(h, h + size)
            at = i * rows
            v = t_dot(normed[:, i * F + half : (i + 1) * F], gg[:, cols]) + got[at : at + half, cols].astype(F32)
            out[:half, cols] = v.astype(out.dtype)
            v = t_dot(normed[:, i * F : (i + 1) * F], gu[:, cols]) + got[at + half : at + rows, cols].astype(F32)
            out[half:, cols] = v.astype(out.dtype)


def keep3_body(got_in, normed, gproj, gm_all, mixin, mine, theirs, got, sems):
    F = mine.shape[0]
    W = mixin.shape[1]
    arrived(pull([(got_in, got)], sems))
    for i, out in enumerate((mine, theirs)):
        rows = slice(i * F, (i + 1) * F)
        for n in range(3):
            cols = slice(n * W, (n + 1) * W)
            out[:, cols] = (t_dot(normed[:, rows], gproj[:, cols]) + got[rows, cols].astype(F32)).astype(out.dtype)
        cols = slice(3 * W, 4 * W)
        out[:, cols] = (t_dot(gm_all[:, rows], mixin[...]) + got[rows, cols].astype(F32)).astype(out.dtype)


def back_body(lengths, *refs):
    gms, rs, wos, (w_in, kernel_in, proj_in, mixin_in, normed_in), rest = split(refs, 4, 4, 4, 5)
    gproj, gm_all, xhat, sent, kernel_part, mixin, normed, wi, edges, back, wo, kernel, xs, proj, sems = rest
    Q = gms[0].shape[0]
    T = 4 * Q
    W = kernel.shape[1]
    DH = wo.shape[1] // 2
    row = lax.broadcasted_iota(jnp.int32, (Q, W), 0)
    soon = pull([(proj_in, proj)], sems)
    tokens = pull([(r, xs.at[j]) for j, r in enumerate(rs)], sems, 1)
    copies = pull(
        laid(gm_all, gms, 0)
        + laid(wo, [w.at[pl.ds(0, W), :] for w in wos], 1)
        + [(kernel_in, kernel), (mixin_in, mixin), (normed_in, normed)],
        sems,
        5,
    )
    weights = pull(blocks_of(wi, w_in), sems, 16)
    arrived(soon)
    edge_products(proj, edges, T, W)
    back[...] = jnp.zeros(back.shape, F32)
    arrived(copies)
    sums = [jnp.zeros((1, W), F32)] * 3
    tail = []
    for j in range(4):
        rows = slice(j * Q, (j + 1) * Q)
        grad_mix = dot_t(gm_all[rows, :], wo[...])
        taps = chunk_taps(lengths, j, 4 * Q, Q, W)
        lags = tapped_lags(proj, edges, taps, j, Q, W)
        conv = kernel[0:1, :] * lags[0] + kernel[1:2, :] * lags[1] + kernel[2:3, :] * lags[2]
        grad_conv = (grad_mix * proj[rows, W : 2 * W]).astype(BF).astype(F32)
        sums = [s + jnp.sum(grad_conv * lag, axis=0, keepdims=True) for s, lag in zip(sums, lags)]
        m0, m1, m2 = [jnp.where(tap, grad_conv, 0.0) for tap in taps]
        m1 = kernel[1:2, :] * m1
        m2 = kernel[2:3, :] * m2
        grad_bv = kernel[0:1, :] * m0
        grad_bv = grad_bv + jnp.where(row < Q - 1, pltpu.roll(m1, Q - 1, 0), 0.0)
        grad_bv = grad_bv + jnp.where(row < Q - 2, pltpu.roll(m2, Q - 2, 0), 0.0)
        head = lax.broadcasted_iota(jnp.int32, (EDGE, W), 0)
        last = jnp.where(head == EDGE - 1, m1[0:1] + m2[1:2], 0.0)
        back[neighbour(j)] = jnp.where(head == EDGE - 2, m2[0:1], last)
        gproj[rows, :W] = (grad_bv * proj[rows, 2 * W :]).astype(BF)
        gproj[rows, W : 2 * W] = (grad_mix * conv).astype(BF)
        gproj[rows, 2 * W :] = (grad_bv * proj[rows, :W]).astype(BF)
    for i in range(3):
        kernel_part[i : i + 1, :] = sums[i]
    for j in range(4):
        lo = T + j * EDGE
        tail.append(
            jnp.concatenate(
                [back[j] * proj[lo : lo + EDGE, 2 * W :], jnp.zeros((EDGE, W), F32), back[j] * proj[lo : lo + EDGE, :W]],
                axis=1,
            )
        )
    gproj[T:, :] = jnp.concatenate(tail, axis=0).astype(BF)
    for i in range(3):
        cols = slice(i * W, (i + 1) * W)
        sent[:, cols] = t_dot(normed[:, DH:], gproj[:, cols]).astype(BF)
    sent[:, 3 * W :] = t_dot(gm_all[:, DH:], mixin[...]).astype(BF)
    for j in range(4):
        tokens[j].wait()
        v = xs[j, : Q + EDGE, :].astype(F32)
        v = v * lax.rsqrt(jnp.mean(v * v, axis=1, keepdims=True) + EPS)
        xhat[j * Q : (j + 1) * Q, :] = v[:Q]
        xhat[T + j * EDGE : T + (j + 1) * EDGE, :] = v[Q:]
    arrived(weights)


def last_body(w, gproj, xhat, norm2, own, s1, s2, s3, norms):
    D = own.shape[1]
    Q = own.shape[0] - 2 * EDGE
    T = 4 * Q
    head = lax.broadcasted_iota(jnp.int32, (EDGE, D // 4), 0)
    for n in range(0, D, D // 4):
        cols = slice(n, n + D // 4)
        v = dot_t(gproj[...], w[cols, :])
        one = jnp.sum(v * xhat[:, cols], axis=0, keepdims=True).astype(BF).astype(F32)
        two = norm2[:, cols].astype(BF).astype(F32)
        norms[0:1, cols] = one
        norms[1:2, cols] = two
        more = jnp.where(head == 0, one, jnp.where(head == 1, two, 0.0))
        for k, out in enumerate((own, s1, s2, s3)):
            out[:Q, cols] = v[k * Q : (k + 1) * Q].astype(out.dtype)
            edge = v[T + k * EDGE : T + (k + 1) * EDGE]
            out[Q:, cols] = jnp.concatenate([edge, more], axis=0).astype(out.dtype)


def finish_body(g2, g3, g1, o2, o3, o1, own, x_own, gain, grad_mid, mid_own, out_own, norms, kernel_part, p0, p2, p1, p3, got, got_out, sems):
    Q, D = out_own.shape
    E = Q + EDGE
    F = D // 4
    copies = pull([(g, got.at[i]) for i, g in enumerate((g2, g3, g1))], sems)
    outer = pull([(o, got_out.at[i]) for i, o in enumerate((o2, o3, o1))], sems, 3)
    x = x_own[...].astype(F32)[:E]
    inv = lax.rsqrt(jnp.mean(x * x, axis=1, keepdims=True) + EPS)
    arrived(copies)
    two, three, one = [got[i].astype(F32) for i in range(3)]
    total = (norms[...] + one[E : E + 2]) + (two[E : E + 2] + three[E : E + 2])
    grad = own[:E, :] + two[:E] + three[:E] + one[:E]
    scaled = grad * gain[0:1, :]
    inner = jnp.mean(scaled * x, axis=1, keepdims=True)
    res = inv * scaled - x * (inv * inv * inv * inner)
    arrived(outer)
    out = mid_own[...] + out_own[...]
    for i in range(3):
        out = out + got_out[i].astype(F32)
    main = res[:Q] + grad_mid[...]
    small = jnp.concatenate([total, jnp.zeros((EDGE - 2, D), F32)], axis=0)
    row = lax.broadcasted_iota(jnp.int32, (EDGE, F), 0)
    for i, piece in enumerate((p0, p2, p1, p3)):
        cols = slice(i * F, (i + 1) * F)
        sums = small[:, cols]
        for n in range(3):
            sums = jnp.where(row == 2 + n, kernel_part[n : n + 1, :], sums)
        edge = jnp.concatenate([res[Q:, cols], sums], axis=0)
        piece[:Q, :] = main[:, cols].astype(BF)
        piece[Q : Q + 2 * EDGE, :] = edge.astype(BF)
        piece[Q + 2 * EDGE :, :] = out[:, cols].astype(BF)


def settle_body(p0, p1, p2, p3, grad_ref, out_ref, small, held, sems):
    S = grad_ref.shape[0]
    Q = S // 4
    c = lax.axis_index("cols")
    copies = pull([(p, held.at[k]) for k, p in enumerate((p0, p1, p2, p3))], sems)
    arrived(copies)
    for k in range(4):
        start = pl.multiple_of((c ^ k) * Q, 16)
        grad_ref[pl.ds(start, Q), :] = held[k, :Q].astype(F32)
        out_ref[pl.ds(start, Q), :] = held[k, Q + 2 * EDGE :]
    for k in range(4):
        before = pl.multiple_of(lax.rem((c ^ k) * Q + S - EDGE, S), 8)
        grad_ref[pl.ds(before, EDGE), :] += held[k, Q : Q + 2 * EDGE].astype(F32)[:EDGE]
    s0, s1, s2, s3 = [held[k, Q : Q + 2 * EDGE].astype(F32)[EDGE:] for k in range(4)]
    small[...] = (s0 + s1) + (s2 + s3)


def total_body(twin, other_in, mine, in_ref, out_ref, other, sems):
    W = in_ref.shape[2]
    arrived(pull([(other_in, other)], sems))
    for n in range(4):
        cols = slice(n * W, (n + 1) * W)
        v = mine[:, cols].astype(F32)
        if twin:
            v = v + other[:, cols].astype(F32)
        if n < 3:
            in_ref[:, n, :] = v
        else:
            out_ref[...] = v.T


def local(tokens, lengths, gain1, w_in, kernel, w_out, gain2, w_gu, w_down, cotangent):
    S, F = tokens.shape
    R, C = lax.axis_size("rows"), lax.axis_size("cols")
    assert R == 4 and C == 4
    y = lax.axis_index("dp")
    twin = lax.axis_size("dp") == 2
    Q = S // C
    E = Q + EDGE
    T = R * Q
    TE = R * E
    W = w_out.shape[0]
    H = w_down.shape[0]
    D = C * F
    DH = 2 * F
    half = F // 2

    order = (0, 2, 1, 3)

    def exchange(pieces):
        return [pieces[0]] + [swap(pieces[k], "cols", k) for k in (1, 2, 3)]

    def gather_rows(a):
        far_two = swap(a, "rows", 2)
        far_three = swap(a, "rows", 3)
        return [a, swap(a, "rows", 1), far_two, far_three]

    def over(v):
        return swap(v, "dp", 1)

    def near(*vs):
        return [swap(v, "cols", 1) for v in vs]

    join = lax.optimization_barrier
    vmem = pltpu.VMEM
    mine = E + EDGE

    placed = on_core(
        place_body, [shape((mine + Q, F), BF)] * 4, [vmem((R, 16, F), BF), vmem((2, 1, F), F32)], 14, 60
    )((), (tokens, cotangent, gain1.reshape(1, F), gain2.reshape(1, F)), ())
    pieces = exchange(placed)
    wi_all = lax.all_gather(w_in.reshape(F, 3 * W), "cols", tiled=True)
    wo = after(w_out, placed[0])
    if twin:
        wo = jnp.where(y == 0, wo[:, : F // 2], wo[:, F // 2 :])
    wg = after(w_gu, placed[0]).reshape(F, 2 * H)
    pieces, wo_parts, wg = join((pieces, gather_rows(wo), wg))
    x_own, dy_own, gains = on_core(
        join_body,
        [shape((mine, D), BF), shape((Q, D), BF), shape((2, D), F32)],
        [vmem((C, mine + Q, F), BF)],
        4,
    )((), [pieces[k] for k in order], ())

    parts = gather_rows(x_own)
    wo = cat(wo_parts, 0)
    if twin:
        wo_other = swap(wo, "dp", 1)
        wo = cat([jnp.where(y == 0, wo, wo_other), jnp.where(y == 0, wo_other, wo)], 1)
    wg_half = wg
    if twin:
        wg_half = jnp.where(y == 0, wg[: F // 2], wg[F // 2 :])
    wg_far = swap(after(wg_half, x_own), "cols", 2)
    wd_all = lax.all_gather(after(w_down, x_own), "cols", tiled=True)
    parts = join(parts)
    normed1, proj, mixin = on_core(
        mixer_body,
        [stored((TE, D), BF), stored((TE, 3 * W), F32), stored((T, W), BF)],
        [vmem((TE, D), BF), vmem((TE, 3 * W), F32), vmem((T, W), BF), vmem((R, mine, D), BF), vmem((D, 3 * W), BF)]
        + [vmem((R, EDGE, W), F32), vmem((3, W), F32)],
        15,
        60,
    )((lengths,), (*parts, kernel, wi_all), (gains,))

    mixin, wg_far, wo = join((mixin, wg_far, wo))
    mix_parts = gather_rows(mixin)
    wo_far = swap(wo, "cols", 2)
    wg_fars = [wg_far, swap(wg_far, "dp", 1)] if twin else [wg_far]
    mix_parts, wo_far, wo, wg_fars, wd_all, wg = join((mix_parts, wo_far, wo, wg_fars, wd_all, wg))
    wg_pieces = [wg] + wg_fars + near(wg, *wg_fars)
    wo_pieces = [wo, wo_far] + near(wo, wo_far)

    dy_parts = gather_rows(after(dy_own, mix_parts[1]))
    mid_own, normed2, xhat2, act, slope, silu, wg_here = on_core(
        functools.partial(forward_body, len(wg_pieces)),
        [shape((Q, D), F32), shape((T, D), BF), shape((T, D), F32), shape((T, H), BF), shape((T, H), F32), shape((T, H), F32)]
        + [shape((D, 2 * H), BF)],
        [vmem((R, Q, D), BF), vmem((T, D), F32), vmem((T, D), BF), vmem((D, D), BF)],
        24 + len(wg_pieces),
    )((), (*parts, *mix_parts, *wo_pieces, *wg_pieces), (gains,))
    out_own, o1, o2, o3, wd_here = on_core(
        out_body, [shape((Q, D), F32)] + [shape((Q, D), BF)] * 3 + [shape((H, D), BF)], (), 4
    )((), (wd_all,), (act,))
    dy_parts, o1, o2, o3, wd_here = join((dy_parts, o1, o2, o3, wd_here))

    grad_gate, grad_up, dy_all = on_core(
        turn_body, [shape((T, H), BF)] * 2 + [shape((T, D), BF)], (), 4
    )((), dy_parts, (wd_here, slope, silu))
    gn2_own, t1, t2, t3, norm2_part = on_core(
        through_body, [shape((Q, D), F32)] + [shape((Q, D), BF)] * 3 + [shape((1, D), F32)]
    )((), (), (wg_here, grad_gate, grad_up, xhat2))

    def keep(body, size, got, *arrays):
        return on_core(body, [shape(size, F32), shape(size, BF)], [vmem(got.shape, BF)], 1)((), (got,), arrays)

    def add_far(mine, got):
        return low(mine + got.astype(F32))

    def add_dp(mine, other):
        if twin:
            return mine.astype(F32) + other.astype(F32)
        return lax.psum(mine.astype(F32), "dp")

    def over(v):
        return swap(v, "dp", 1) if twin else v

    third = 3 * half
    t1, t2, t3, grad_gate, grad_up = join((t1, t2, t3, grad_gate, grad_up))
    gn2_got = [swap(t, "rows", k) for k, t in ((2, t2), (3, t3), (1, t1))]
    sent1, sent2 = on_core(sent_body, [shape((third * 2, H), BF)] * 2)(
        (), (), (dy_all, act, normed2, grad_gate, grad_up)
    )
    got1, got2 = near(sent1, sent2)
    mine1, far1 = keep(keep1_body, (third, H), got1, dy_all, act, normed2, grad_gate)
    mine2, far2 = keep(keep2_body, (third, H), got2, normed2, grad_gate, grad_up)
    gn2_got, far1, far2 = join((gn2_got, far1, far2))
    for g in gn2_got:
        gn2_own = gn2_own + g.astype(F32)
    inv2_own = lax.rsqrt(jnp.mean(mid_own * mid_own, axis=1, keepdims=True) + EPS)
    scaled = gn2_own * gains[1:2]
    inner = jnp.mean(scaled * mid_own, axis=1, keepdims=True)
    grad_mid = dy_own.astype(F32) + inv2_own * scaled - mid_own * (inv2_own**3 * inner)

    gm_low, far1 = join((grad_mid.astype(BF), far1))
    gm_parts = gather_rows(gm_low)
    far1 = swap(far1, "cols", 2)
    gm_parts, far1, far2 = join((gm_parts, far1, far2))

    sum1 = add_far(mine1, far1)
    far2 = swap(far2, "cols", 2)
    other1 = over(sum1)
    out_got = [swap(after(o, gm_parts[2]), "rows", k) for k, o in ((2, o2), (3, o3), (1, o1))]
    gproj, gm_all, xhat1, sent3, kernel_part, mixin_here, normed_here, wi_here = on_core(
        back_body,
        [shape((TE, 3 * W), BF), shape((T, D), BF), shape((TE, D), F32), shape((DH, 4 * W), BF), shape((3, W), F32)]
        + [shape((T, W), BF), shape((TE, D), BF), shape((D, 3 * W), BF)],
        [vmem((R, EDGE, W), F32), vmem((R, EDGE, W), F32), vmem((W, D), BF), vmem((3, W), F32)]
        + [vmem((R, mine, D), BF), vmem((TE, 3 * W), F32)],
        20,
    )((lengths,), (*gm_parts, *parts, *wo_pieces, wi_all, kernel, proj, mixin, normed1), ())
    gn1_own, t1, t2, t3, norms = on_core(
        last_body, [shape((mine, D), F32)] + [shape((mine, D), BF)] * 3 + [shape((2, D), F32)]
    )((), (), (wi_here, gproj, xhat1, norm2_part))

    t1, t2, t3, sent3, far2, other1, out_got = join((t1, t2, t3, sent3, far2, other1, out_got))
    sum2 = add_far(mine2, far2)
    (got3,) = near(sent3)
    gn1_got = [swap(t, "rows", k) for k, t in ((2, t2), (3, t3), (1, t1))]
    mine3, far3 = keep(keep3_body, (F, 4 * W), got3, normed_here, gproj, gm_all, mixin_here)
    far3 = swap(far3, "cols", 2)
    other2 = over(sum2)
    total1 = add_dp(sum1, other1)
    down_grad = total1[:F].T
    gn1_got, far3, other2, down_grad = join((gn1_got, far3, other2, down_grad))
    sum3 = add_far(mine3, far3)
    other3 = over(sum3)

    norms = after(norms, sum3)
    sends = on_core(
        finish_body, [shape((mine + Q, F), BF)] * 4, [vmem((3, mine, D), BF), vmem((3, Q, D), BF)], 6
    )((), (*gn1_got, *out_got), (gn1_own, x_own, gains, grad_mid, mid_own, out_own, norms, kernel_part))
    got = exchange([sends[order.index(k)] for k in range(C)])
    input_grad, block_output, small = on_core(
        settle_body,
        [shape((S, F), F32), shape((S, F), BF), shape((EDGE, F), F32)],
        [vmem((C, mine + Q, F), BF)],
        4,
    )((), got, ())
    small = add_dp(small, over(small))

    sum2, other2 = after((sum2, other2), got[1])
    total2 = add_dp(sum2, other2)
    gu_grad = jnp.stack([cat([total1[F:], total2[:half]], 0), total2[half:]], axis=1)
    if not twin:
        sum3 = lax.psum(sum3.astype(F32), "dp")
        other3 = sum3
    in_grad, out_grad = on_core(
        functools.partial(total_body, twin),
        [shape((F, 3, W), F32), shape((W, F), F32)],
        [vmem(other3.shape, other3.dtype)],
        1,
    )((), (other3,), (sum3,))
    return (
        block_output,
        input_grad,
        small[0],
        in_grad,
        small[2:5],
        out_grad,
        small[1],
        gu_grad,
        down_grad,
    )


def solution(mesh):
    tok = P(("dp", "rows"), "cols")
    feat = P("cols")
    wide = P("cols", None, "rows")
    tall = P("rows", "cols")
    taps = P(None, "rows")
    return jax.shard_map(
        local,
        mesh=mesh,
        in_specs=(tok, P("dp", None), feat, wide, taps, tall, feat, wide, tall, tok),
        out_specs=(tok, tok, feat, wide, taps, tall, feat, wide, tall),
        check_vma=False,
    )
```

```python
import functools

import jax
import jax.numpy as jnp
from jax import lax
from jax.experimental import pallas as pl
from jax.experimental.pallas import tpu as pltpu
from jax.sharding import PartitionSpec as P

EPS = 1e-06
BF = jnp.bfloat16
F32 = jnp.float32
EDGE = 8


def swap(value, axis, bit):
    size = lax.axis_size(axis)
    return lax.ppermute(value, axis, [(i, i ^ bit) for i in range(size)])


def dot(a, b):
    return jnp.dot(a, b, preferred_element_type=F32)


def dot_t(a, b):
    return lax.dot_general(a, b, (((1,), (1,)), ((), ())), preferred_element_type=F32)


def t_dot(a, b):
    return lax.dot_general(a, b, (((0,), (0,)), ((), ())), preferred_element_type=F32)


def low(v):
    return lax.reduce_precision(v, 8, 7).astype(BF)


def after(value, *first):
    return lax.optimization_barrier((value,) + first)[0]


def cat(parts, dim):
    return jnp.concatenate(parts, axis=dim)


def on_core(body, out, scratch=(), copies=0, limit=24):
    vmem, away = pl.BlockSpec(memory_space=pltpu.VMEM), pl.BlockSpec(memory_space=pltpu.HBM)

    def call(scalars, far, near):
        return pl.pallas_call(
            body,
            out_shape=[o[0] if isinstance(o, tuple) else o for o in out],
            in_specs=[pl.BlockSpec(memory_space=pltpu.SMEM)] * len(scalars)
            + [away] * len(far)
            + [vmem] * len(near),
            out_specs=[away if isinstance(o, tuple) else vmem for o in out],
            scratch_shapes=list(scratch) + ([pltpu.SemaphoreType.DMA((copies,))] if copies else []),
            compiler_params=pltpu.CompilerParams(vmem_limit_bytes=limit * 2**20),
            cost_estimate=pl.CostEstimate(flops=0, bytes_accessed=2**16, transcendentals=0),
        )(*scalars, *far, *near)

    return call


def pull(pairs, sems, first=0):
    started = []
    for i, (source, target) in enumerate(pairs):
        copy = pltpu.make_async_copy(source, target, sems.at[first + i])
        copy.start()
        started.append(copy)
    return started


def arrived(copies):
    for copy in copies:
        copy.wait()


def laid(target, pieces, dim):
    pairs, at = [], 0
    for piece in pieces:
        size = piece.shape[dim]
        place = target.at[pl.ds(at, size), :] if dim == 0 else target.at[:, pl.ds(at, size)]
        pairs.append((piece, place))
        at += size
    return pairs


def shape(dims, kind):
    return jax.ShapeDtypeStruct(dims, kind)


def stored(dims, kind):
    return (shape(dims, kind),)


def place_body(tokens, cotangent, gain1, gain2, p0, p1, p2, p3, edges, gains, sems):
    S = tokens.shape[0]
    Q = S // 4
    mine = Q + 2 * EDGE
    c = lax.axis_index("cols")
    outs = (p0, p1, p2, p3)
    soon = [(gain1, gains.at[0]), (gain2, gains.at[1])]
    later = []
    for k in range(4):
        start = pl.multiple_of((c ^ k) * Q, 16)
        early = pl.multiple_of(lax.rem(start + S - 16, S), 16)
        soon.append((tokens.at[pl.ds(early, 16), :], edges.at[k]))
        later.append((tokens.at[pl.ds(start, Q), :], outs[k].at[pl.ds(0, Q), :]))
        later.append((cotangent.at[pl.ds(start, Q), :], outs[k].at[pl.ds(mine, Q), :]))
    soon = pull(soon, sems)
    later = pull(later, sems, len(soon))
    arrived(soon)
    rows = lax.broadcasted_iota(jnp.int32, (EDGE, tokens.shape[1]), 0)
    values = jnp.zeros(rows.shape, F32)
    at = 0
    for i in range(2):
        left = gains[i]
        for _ in range(3):
            part = left.astype(BF).astype(F32)
            left = left - part
            values = jnp.where(rows == at, part, values)
            at += 1
    for k in range(4):
        edge = edges[k].astype(F32)[16 - EDGE :]
        outs[k][Q:mine, :] = jnp.concatenate([edge, values], axis=0).astype(BF)
    arrived(later)


def join_body(p0, p2, p1, p3, x_ref, dy_ref, g_ref, held, sems):
    F = p0.shape[1]
    Q = dy_ref.shape[0]
    copies = pull([(p, held.at[i]) for i, p in enumerate((p0, p2, p1, p3))], sems)
    for i, copy in enumerate(copies):
        copy.wait()
        cols = slice(i * F, (i + 1) * F)
        x_ref[:, cols] = held[i, : Q + 2 * EDGE]
        dy_ref[:, cols] = held[i, Q + 2 * EDGE :]
        t = held[i, Q : Q + 2 * EDGE].astype(F32)[EDGE:]
        g_ref[0:1, cols] = (t[0:1] + t[1:2]) + t[2:3]
        g_ref[1:2, cols] = (t[3:4] + t[4:5]) + t[5:6]


def chunk_taps(lengths, j, S, Q, W):
    z, c = lax.axis_index("rows"), lax.axis_index("cols")
    place = (z ^ j) * S + c * Q + lax.broadcasted_iota(jnp.int32, (Q, W), 0)
    end = jnp.int32(0)
    start = jnp.zeros_like(place)
    for i in range(lengths.shape[1]):
        end = end + lengths[0, i]
        start = jnp.where(place >= end, end, start)
    return [jnp.logical_and(place < end, place - start >= lag) for lag in range(3)]


def neighbour(j):
    z, c = lax.axis_index("rows"), lax.axis_index("cols")
    return jnp.where(c == 0, lax.rem((z ^ j) + 3, 4) ^ z, j)


def edge_products(proj_ref, edges, T, W):
    for j in range(4):
        lo = T + j * EDGE
        edges[j] = (proj_ref[lo : lo + EDGE, :W] * proj_ref[lo : lo + EDGE, 2 * W :]).astype(BF).astype(F32)


def tapped_lags(proj_ref, edges, taps, j, Q, W):
    lo = j * Q
    bv = (proj_ref[lo : lo + Q, :W] * proj_ref[lo : lo + Q, 2 * W :]).astype(BF).astype(F32)
    edge = edges[neighbour(j)]
    row = lax.broadcasted_iota(jnp.int32, (Q, W), 0)
    one = jnp.where(row == 0, edge[EDGE - 1 :], pltpu.roll(bv, 1, 0))
    two = pltpu.roll(bv, 2, 0)
    two = jnp.where(row == 0, edge[EDGE - 2 : EDGE - 1], jnp.where(row == 1, edge[EDGE - 1 :], two))
    return [jnp.where(tap, lagged, 0.0) for tap, lagged in zip(taps, (bv, one, two))]


def blocks_of(target, gathered, dim=0):
    c = lax.axis_index("cols")
    size = gathered.shape[0] // 4
    pairs = []
    for i, k in enumerate((0, 2, 1, 3)):
        width = gathered.shape[1]
        place = target.at[:, pl.ds(i * width, width)] if dim else target.at[pl.ds(i * size, size), :]
        start = pl.multiple_of((c ^ k) * size, 16)
        pairs.append((gathered.at[pl.ds(start, size), :], place))
    return pairs


def halved(target, pieces):
    if len(pieces) == 4:
        return laid(target, pieces, 0)
    y = lax.axis_index("dp")
    size = pieces[0].shape[0]
    half = size // 2
    pairs = []
    for h in range(2):
        own, first, second = pieces[3 * h : 3 * h + 3]
        base = 2 * size * h
        pairs.append((own, target.at[pl.ds(base, size), :]))
        for piece, at in ((first, y), (second, 1 - y)):
            start = pl.multiple_of(base + size + at * half, 16)
            pairs.append((piece, target.at[pl.ds(start, half), :]))
    return pairs


def split(refs, *counts):
    out = []
    for n in counts:
        out.append(refs[:n])
        refs = refs[n:]
    return out + [refs]


def mixer_body(lengths, r0, r1, r2, r3, kernel_in, w_in, gain, *refs):
    outs, (normed, proj, mixin, xs, w, edges, kernel, sems) = split(refs, 3)
    Q = xs.shape[1] - 2 * EDGE
    T = 4 * Q
    W = kernel.shape[1]
    tokens = pull([(r, xs.at[j]) for j, r in enumerate((r0, r1, r2, r3))], sems)
    tokens += pull([(kernel_in, kernel)], sems, 4)
    weights = pull(blocks_of(w, w_in), sems, 5)
    tail = []
    for j in range(4):
        tokens[j].wait()
        v = xs[j, : Q + EDGE, :].astype(F32)
        inv = lax.rsqrt(jnp.mean(v * v, axis=1, keepdims=True) + EPS)
        n = v * inv * gain[0:1, :]
        normed[j * Q : (j + 1) * Q, :] = n[:Q].astype(BF)
        tail.append(n[Q:])
    normed[T:, :] = jnp.concatenate(tail, axis=0).astype(BF)
    out = pull([(normed, outs[0])], sems, 9)
    arrived(weights + tokens[4:])
    for i in range(3):
        cols = slice(i * W, (i + 1) * W)
        proj[:, cols] = dot(normed[...], w[:, cols])
    out += pull([(proj, outs[1])], sems, 10)
    edge_products(proj, edges, T, W)
    for j in range(4):
        taps = chunk_taps(lengths, j, 4 * Q, Q, W)
        lags = tapped_lags(proj, edges, taps, j, Q, W)
        conv = kernel[0:1, :] * lags[0] + kernel[1:2, :] * lags[1] + kernel[2:3, :] * lags[2]
        rows = slice(j * Q, (j + 1) * Q)
        mixin[rows, :] = (proj[rows, W : 2 * W] * conv).astype(BF)
        out += pull([(mixin.at[pl.ds(j * Q, Q), :], outs[2].at[pl.ds(j * Q, Q), :])], sems, 11 + j)
    arrived(out)


def hidden_tiles(H):
    return [(h, min(256, H - h)) for h in range(0, H, 256)]


def forward_body(ng, *refs):
    rs, ms, wos, wgs, (gain,), rest = split(refs, 4, 4, 4, ng, 1)
    mid_own, normed, xhat, act, slope, silu_ref, wg, xs, mid, mix, wo, sems = rest
    T, W = ms[0].shape
    Q = T // 4
    H = act.shape[1]
    gain2 = gain[1:2, :]
    tokens = [(r.at[pl.ds(0, Q), :], xs.at[j]) for j, r in enumerate(rs)]
    blocks = [
        (ms[k].at[pl.ds((j ^ k) * Q, Q), :], mix.at[pl.ds(j * Q, Q), pl.ds(k * W, W)])
        for j in range(4)
        for k in range(4)
    ]
    outs = pull(laid(wo, wos, 1), sems)
    blocks = pull(blocks, sems, 4)
    tokens = pull(tokens, sems, 20)
    wide = pull(halved(wg, wgs), sems, 24)
    arrived(outs)
    for j in range(4):
        arrived(blocks[4 * j : 4 * j + 4])
        tokens[j].wait()
        rows = slice(j * Q, (j + 1) * Q)
        mid[rows, :] = xs[j].astype(F32) + dot(mix[rows, :], wo[...])
        v = mid[rows, :]
        inv = lax.rsqrt(jnp.mean(v * v, axis=1, keepdims=True) + EPS)
        xhat[rows, :] = v * inv
        normed[rows, :] = (v * inv * gain2).astype(BF)
    mid_own[...] = mid[:Q, :]
    arrived(wide)
    for h, size in hidden_tiles(H):
        cols, ups = slice(h, h + size), slice(H + h, H + h + size)
        gate = dot(normed[...], wg[:, cols])
        up = dot(normed[...], wg[:, ups])
        sig = 1.0 / (1.0 + jnp.exp(-gate))
        silu = gate * sig
        act[:, cols] = (silu * up).astype(BF)
        silu_ref[:, cols] = silu
        slope[:, cols] = up * sig * (1.0 + gate * (1.0 - sig))


def out_body(w_down, act, own, s1, s2, s3, wd, sems):
    Q, D = own.shape
    copies = pull(blocks_of(wd, w_down, 1), sems)
    for i, n in enumerate(range(0, D, D // 4)):
        cols = slice(n, n + D // 4)
        copies[i].wait()
        v = dot(act[...], wd[:, cols])
        own[:, cols] = v[:Q]
        for k, out in ((1, s1), (2, s2), (3, s3)):
            out[:, cols] = v[k * Q : (k + 1) * Q].astype(BF)


def turn_body(r0, r1, r2, r3, wd, slope, silu, gg, gu, dy_all, sems):
    H = gg.shape[1]
    arrived(pull(laid(dy_all, (r0, r1, r2, r3), 0), sems))
    for h, size in hidden_tiles(H):
        cols = slice(h, h + size)
        grad = dot_t(dy_all[...], wd[cols, :])
        gu[:, cols] = (grad * silu[:, cols]).astype(BF)
        gg[:, cols] = (grad * slope[:, cols]).astype(BF)


def sent_body(dy_all, act, normed, gg, gu, sent1, sent2):
    F = dy_all.shape[1] // 4
    H = act.shape[1]
    half = F // 2
    for i in range(2):
        at, to = (2 + i) * F, 3 * half * i
        for h, size in hidden_tiles(H):
            cols = slice(h, h + size)
            sent1[to : to + F, cols] = t_dot(dy_all[:, at : at + F], act[:, cols]).astype(BF)
            v = t_dot(normed[:, at : at + F], gg[:, cols]).astype(BF)
            sent1[to + F : to + 3 * half, cols] = v[:half]
            sent2[to : to + half, cols] = v[half:]
            sent2[to + half : to + 3 * half, cols] = t_dot(normed[:, at : at + F], gu[:, cols]).astype(BF)


def through_body(wg, gg, gu, xhat, own, s1, s2, s3, norm_part):
    Q, D = own.shape
    H = gg.shape[1]
    for n in range(0, D, D // 4):
        cols = slice(n, n + D // 4)
        v = dot_t(gg[...], wg[cols, :H]) + dot_t(gu[...], wg[cols, H:])
        norm_part[0:1, cols] = jnp.sum(v * xhat[:, cols], axis=0, keepdims=True)
        own[:, cols] = v[:Q]
        for k, out in ((1, s1), (2, s2), (3, s3)):
            out[:, cols] = v[k * Q : (k + 1) * Q].astype(BF)


def keep1_body(got_in, dy_all, act, normed, gg, mine, theirs, got, sems):
    rows = mine.shape[0]
    F = 2 * rows // 3
    half = F // 2
    H = act.shape[1]
    arrived(pull([(got_in, got)], sems))
    for i, out in enumerate((mine, theirs)):
        for h, size in hidden_tiles(H):
            cols = slice(h, h + size)
            v = t_dot(dy_all[:, i * F : (i + 1) * F], act[:, cols]) + got[i * rows : i * rows + F, cols].astype(F32)
            out[:F, cols] = v.astype(out.dtype)
            v = t_dot(normed[:, i * F : i * F + half], gg[:, cols]) + got[i * rows + F : (i + 1) * rows, cols].astype(F32)
            out[F:, cols] = v.astype(out.dtype)


def keep2_body(got_in, normed, gg, gu, mine, theirs, got, sems):
    rows = mine.shape[0]
    F = 2 * rows // 3
    half = F // 2
    H = gg.shape[1]
    arrived(pull([(got_in, got)], sems))
    for i, out in enumerate((mine, theirs)):
        for h, size in hidden_tiles(H):
            cols = slice(h, h + size)
            at = i * rows
            v = t_dot(normed[:, i * F + half : (i + 1) * F], gg[:, cols]) + got[at : at + half, cols].astype(F32)
            out[:half, cols] = v.astype(out.dtype)
            v = t_dot(normed[:, i * F : (i + 1) * F], gu[:, cols]) + got[at + half : at + rows, cols].astype(F32)
            out[half:, cols] = v.astype(out.dtype)


def keep3_body(got_in, normed, gproj, gm_all, mixin, mine, theirs, got, sems):
    F = mine.shape[0]
    W = mixin.shape[1]
    arrived(pull([(got_in, got)], sems))
    for i, out in enumerate((mine, theirs)):
        rows = slice(i * F, (i + 1) * F)
        for n in range(3):
            cols = slice(n * W, (n + 1) * W)
            out[:, cols] = (t_dot(normed[:, rows], gproj[:, cols]) + got[rows, cols].astype(F32)).astype(out.dtype)
        cols = slice(3 * W, 4 * W)
        out[:, cols] = (t_dot(gm_all[:, rows], mixin[...]) + got[rows, cols].astype(F32)).astype(out.dtype)


def back_body(lengths, *refs):
    gms, rs, wos, (w_in, kernel_in, proj_in, mixin_in, normed_in), rest = split(refs, 4, 4, 4, 5)
    gproj, gm_all, xhat, sent, kernel_part, mixin, normed, wi, edges, back, wo, kernel, xs, proj, sems = rest
    Q = gms[0].shape[0]
    T = 4 * Q
    W = kernel.shape[1]
    DH = wo.shape[1] // 2
    row = lax.broadcasted_iota(jnp.int32, (Q, W), 0)
    soon = pull([(proj_in, proj)], sems)
    tokens = pull([(r, xs.at[j]) for j, r in enumerate(rs)], sems, 1)
    copies = pull(
        laid(gm_all, gms, 0)
        + laid(wo, [w.at[pl.ds(0, W), :] for w in wos], 1)
        + [(kernel_in, kernel), (mixin_in, mixin), (normed_in, normed)],
        sems,
        5,
    )
    weights = pull(blocks_of(wi, w_in), sems, 16)
    arrived(soon)
    edge_products(proj, edges, T, W)
    back[...] = jnp.zeros(back.shape, F32)
    arrived(copies)
    sums = [jnp.zeros((1, W), F32)] * 3
    tail = []
    for j in range(4):
        rows = slice(j * Q, (j + 1) * Q)
        grad_mix = dot_t(gm_all[rows, :], wo[...])
        taps = chunk_taps(lengths, j, 4 * Q, Q, W)
        lags = tapped_lags(proj, edges, taps, j, Q, W)
        conv = kernel[0:1, :] * lags[0] + kernel[1:2, :] * lags[1] + kernel[2:3, :] * lags[2]
        grad_conv = (grad_mix * proj[rows, W : 2 * W]).astype(BF).astype(F32)
        sums = [s + jnp.sum(grad_conv * lag, axis=0, keepdims=True) for s, lag in zip(sums, lags)]
        m0, m1, m2 = [jnp.where(tap, grad_conv, 0.0) for tap in taps]
        m1 = kernel[1:2, :] * m1
        m2 = kernel[2:3, :] * m2
        grad_bv = kernel[0:1, :] * m0
        grad_bv = grad_bv + jnp.where(row < Q - 1, pltpu.roll(m1, Q - 1, 0), 0.0)
        grad_bv = grad_bv + jnp.where(row < Q - 2, pltpu.roll(m2, Q - 2, 0), 0.0)
        head = lax.broadcasted_iota(jnp.int32, (EDGE, W), 0)
        last = jnp.where(head == EDGE - 1, m1[0:1] + m2[1:2], 0.0)
        back[neighbour(j)] = jnp.where(head == EDGE - 2, m2[0:1], last)
        gproj[rows, :W] = (grad_bv * proj[rows, 2 * W :]).astype(BF)
        gproj[rows, W : 2 * W] = (grad_mix * conv).astype(BF)
        gproj[rows, 2 * W :] = (grad_bv * proj[rows, :W]).astype(BF)
    for i in range(3):
        kernel_part[i : i + 1, :] = sums[i]
    for j in range(4):
        lo = T + j * EDGE
        tail.append(
            jnp.concatenate(
                [back[j] * proj[lo : lo + EDGE, 2 * W :], jnp.zeros((EDGE, W), F32), back[j] * proj[lo : lo + EDGE, :W]],
                axis=1,
            )
        )
    gproj[T:, :] = jnp.concatenate(tail, axis=0).astype(BF)
    for i in range(3):
        cols = slice(i * W, (i + 1) * W)
        sent[:, cols] = t_dot(normed[:, DH:], gproj[:, cols]).astype(BF)
    sent[:, 3 * W :] = t_dot(gm_all[:, DH:], mixin[...]).astype(BF)
    for j in range(4):
        tokens[j].wait()
        v = xs[j, : Q + EDGE, :].astype(F32)
        v = v * lax.rsqrt(jnp.mean(v * v, axis=1, keepdims=True) + EPS)
        xhat[j * Q : (j + 1) * Q, :] = v[:Q]
        xhat[T + j * EDGE : T + (j + 1) * EDGE, :] = v[Q:]
    arrived(weights)


def last_body(w, gproj, xhat, norm2, own, s1, s2, s3, norms):
    D = own.shape[1]
    Q = own.shape[0] - 2 * EDGE
    T = 4 * Q
    head = lax.broadcasted_iota(jnp.int32, (EDGE, D // 4), 0)
    for n in range(0, D, D // 4):
        cols = slice(n, n + D // 4)
        v = dot_t(gproj[...], w[cols, :])
        one = jnp.sum(v * xhat[:, cols], axis=0, keepdims=True).astype(BF).astype(F32)
        two = norm2[:, cols].astype(BF).astype(F32)
        norms[0:1, cols] = one
        norms[1:2, cols] = two
        more = jnp.where(head == 0, one, jnp.where(head == 1, two, 0.0))
        for k, out in enumerate((own, s1, s2, s3)):
            out[:Q, cols] = v[k * Q : (k + 1) * Q].astype(out.dtype)
            edge = v[T + k * EDGE : T + (k + 1) * EDGE]
            out[Q:, cols] = jnp.concatenate([edge, more], axis=0).astype(out.dtype)


def finish_body(g2, g3, g1, o2, o3, o1, own, x_own, gain, grad_mid, mid_own, out_own, norms, kernel_part, p0, p2, p1, p3, got, got_out, sems):
    Q, D = out_own.shape
    E = Q + EDGE
    F = D // 4
    copies = pull([(g, got.at[i]) for i, g in enumerate((g2, g3, g1))], sems)
    outer = pull([(o, got_out.at[i]) for i, o in enumerate((o2, o3, o1))], sems, 3)
    x = x_own[...].astype(F32)[:E]
    inv = lax.rsqrt(jnp.mean(x * x, axis=1, keepdims=True) + EPS)
    arrived(copies)
    two, three, one = [got[i].astype(F32) for i in range(3)]
    total = (norms[...] + one[E : E + 2]) + (two[E : E + 2] + three[E : E + 2])
    grad = own[:E, :] + two[:E] + three[:E] + one[:E]
    scaled = grad * gain[0:1, :]
    inner = jnp.mean(scaled * x, axis=1, keepdims=True)
    res = inv * scaled - x * (inv * inv * inv * inner)
    arrived(outer)
    out = mid_own[...] + out_own[...]
    for i in range(3):
        out = out + got_out[i].astype(F32)
    main = res[:Q] + grad_mid[...]
    small = jnp.concatenate([total, jnp.zeros((EDGE - 2, D), F32)], axis=0)
    row = lax.broadcasted_iota(jnp.int32, (EDGE, F), 0)
    for i, piece in enumerate((p0, p2, p1, p3)):
        cols = slice(i * F, (i + 1) * F)
        sums = small[:, cols]
        for n in range(3):
            sums = jnp.where(row == 2 + n, kernel_part[n : n + 1, :], sums)
        edge = jnp.concatenate([res[Q:, cols], sums], axis=0)
        piece[:Q, :] = main[:, cols].astype(BF)
        piece[Q : Q + 2 * EDGE, :] = edge.astype(BF)
        piece[Q + 2 * EDGE :, :] = out[:, cols].astype(BF)


def settle_body(p0, p1, p2, p3, grad_ref, out_ref, small, held, sems):
    S = grad_ref.shape[0]
    Q = S // 4
    c = lax.axis_index("cols")
    copies = pull([(p, held.at[k]) for k, p in enumerate((p0, p1, p2, p3))], sems)
    arrived(copies)
    for k in range(4):
        start = pl.multiple_of((c ^ k) * Q, 16)
        grad_ref[pl.ds(start, Q), :] = held[k, :Q].astype(F32)
        out_ref[pl.ds(start, Q), :] = held[k, Q + 2 * EDGE :]
    for k in range(4):
        before = pl.multiple_of(lax.rem((c ^ k) * Q + S - EDGE, S), 8)
        grad_ref[pl.ds(before, EDGE), :] += held[k, Q : Q + 2 * EDGE].astype(F32)[:EDGE]
    s0, s1, s2, s3 = [held[k, Q : Q + 2 * EDGE].astype(F32)[EDGE:] for k in range(4)]
    small[...] = (s0 + s1) + (s2 + s3)


def total_body(twin, other_in, mine, small, more, in_ref, out_ref, n1_ref, n2_ref, kernel_ref, other, sems):
    W = in_ref.shape[2]
    copies = pull([(other_in, other)], sems)
    sums = small[...] + more[...] if twin else small[...]
    n1_ref[...] = sums[0:1]
    n2_ref[...] = sums[1:2]
    kernel_ref[...] = sums[2:5]
    arrived(copies)
    for n in range(4):
        cols = slice(n * W, (n + 1) * W)
        v = mine[:, cols].astype(F32)
        if twin:
            v = v + other[:, cols].astype(F32)
        if n < 3:
            in_ref[:, n, :] = v
        else:
            out_ref[...] = v.T


def local(tokens, lengths, gain1, w_in, kernel, w_out, gain2, w_gu, w_down, cotangent):
    S, F = tokens.shape
    R, C = lax.axis_size("rows"), lax.axis_size("cols")
    assert R == 4 and C == 4
    y = lax.axis_index("dp")
    twin = lax.axis_size("dp") == 2
    Q = S // C
    E = Q + EDGE
    T = R * Q
    TE = R * E
    W = w_out.shape[0]
    H = w_down.shape[0]
    D = C * F
    DH = 2 * F
    half = F // 2

    order = (0, 2, 1, 3)

    def exchange(pieces):
        return [pieces[0]] + [swap(pieces[k], "cols", k) for k in (1, 2, 3)]

    def gather_rows(a):
        far_two = swap(a, "rows", 2)
        far_three = swap(a, "rows", 3)
        return [a, swap(a, "rows", 1), far_two, far_three]

    def over(v):
        return swap(v, "dp", 1)

    def near(*vs):
        return [swap(v, "cols", 1) for v in vs]

    join = lax.optimization_barrier
    vmem = pltpu.VMEM
    mine = E + EDGE

    placed = on_core(
        place_body, [shape((mine + Q, F), BF)] * 4, [vmem((R, 16, F), BF), vmem((2, 1, F), F32)], 14, 60
    )((), (tokens, cotangent, gain1.reshape(1, F), gain2.reshape(1, F)), ())
    pieces = exchange(placed)
    wi_all = lax.all_gather(w_in.reshape(F, 3 * W), "cols", tiled=True)
    wo = after(w_out, placed[0])
    if twin:
        wo = jnp.where(y == 0, wo[:, : F // 2], wo[:, F // 2 :])
    wg = after(w_gu, placed[0]).reshape(F, 2 * H)
    pieces, wo_parts, wg = join((pieces, gather_rows(wo), wg))
    x_own, dy_own, gains = on_core(
        join_body,
        [shape((mine, D), BF), shape((Q, D), BF), shape((2, D), F32)],
        [vmem((C, mine + Q, F), BF)],
        4,
    )((), [pieces[k] for k in order], ())

    parts = gather_rows(x_own)
    wo = cat(wo_parts, 0)
    if twin:
        wo_other = swap(wo, "dp", 1)
        wo = cat([jnp.where(y == 0, wo, wo_other), jnp.where(y == 0, wo_other, wo)], 1)
    wg_half = wg
    if twin:
        wg_half = jnp.where(y == 0, wg[: F // 2], wg[F // 2 :])
    wg_far = swap(after(wg_half, x_own), "cols", 2)
    wd_all = lax.all_gather(after(w_down, x_own), "cols", tiled=True)
    parts = join(parts)
    normed1, proj, mixin = on_core(
        mixer_body,
        [stored((TE, D), BF), stored((TE, 3 * W), F32), stored((T, W), BF)],
        [vmem((TE, D), BF), vmem((TE, 3 * W), F32), vmem((T, W), BF), vmem((R, mine, D), BF), vmem((D, 3 * W), BF)]
        + [vmem((R, EDGE, W), F32), vmem((3, W), F32)],
        15,
        60,
    )((lengths,), (*parts, kernel, wi_all), (gains,))

    mixin, wg_far, wo = join((mixin, wg_far, wo))
    mix_parts = gather_rows(mixin)
    wo_far = swap(wo, "cols", 2)
    wg_fars = [wg_far, swap(wg_far, "dp", 1)] if twin else [wg_far]
    mix_parts, wo_far, wo, wg_fars, wd_all, wg = join((mix_parts, wo_far, wo, wg_fars, wd_all, wg))
    wg_pieces = [wg] + wg_fars + near(wg, *wg_fars)
    wo_pieces = [wo, wo_far] + near(wo, wo_far)

    dy_parts = gather_rows(after(dy_own, mix_parts[1]))
    mid_own, normed2, xhat2, act, slope, silu, wg_here = on_core(
        functools.partial(forward_body, len(wg_pieces)),
        [shape((Q, D), F32), shape((T, D), BF), shape((T, D), F32), shape((T, H), BF), shape((T, H), F32), shape((T, H), F32)]
        + [shape((D, 2 * H), BF)],
        [vmem((R, Q, D), BF), vmem((T, D), F32), vmem((T, D), BF), vmem((D, D), BF)],
        24 + len(wg_pieces),
    )((), (*parts, *mix_parts, *wo_pieces, *wg_pieces), (gains,))
    out_own, o1, o2, o3, wd_here = on_core(
        out_body, [shape((Q, D), F32)] + [shape((Q, D), BF)] * 3 + [shape((H, D), BF)], (), 4
    )((), (wd_all,), (act,))
    dy_parts, o1, o2, o3, wd_here = join((dy_parts, o1, o2, o3, wd_here))

    grad_gate, grad_up, dy_all = on_core(
        turn_body, [shape((T, H), BF)] * 2 + [shape((T, D), BF)], (), 4
    )((), dy_parts, (wd_here, slope, silu))
    gn2_own, t1, t2, t3, norm2_part = on_core(
        through_body, [shape((Q, D), F32)] + [shape((Q, D), BF)] * 3 + [shape((1, D), F32)]
    )((), (), (wg_here, grad_gate, grad_up, xhat2))

    def keep(body, size, got, *arrays):
        return on_core(body, [shape(size, F32), shape(size, BF)], [vmem(got.shape, BF)], 1)((), (got,), arrays)

    def add_far(mine, got):
        return low(mine + got.astype(F32))

    def add_dp(mine, other):
        if twin:
            return mine.astype(F32) + other.astype(F32)
        return lax.psum(mine.astype(F32), "dp")

    def over(v):
        return swap(v, "dp", 1) if twin else v

    third = 3 * half
    t1, t2, t3, grad_gate, grad_up = join((t1, t2, t3, grad_gate, grad_up))
    gn2_got = [swap(t, "rows", k) for k, t in ((2, t2), (3, t3), (1, t1))]
    sent1, sent2 = on_core(sent_body, [shape((third * 2, H), BF)] * 2)(
        (), (), (dy_all, act, normed2, grad_gate, grad_up)
    )
    got1, got2 = near(sent1, sent2)
    mine1, far1 = keep(keep1_body, (third, H), got1, dy_all, act, normed2, grad_gate)
    mine2, far2 = keep(keep2_body, (third, H), got2, normed2, grad_gate, grad_up)
    gn2_got, far1, far2 = join((gn2_got, far1, far2))
    for g in gn2_got:
        gn2_own = gn2_own + g.astype(F32)
    inv2_own = lax.rsqrt(jnp.mean(mid_own * mid_own, axis=1, keepdims=True) + EPS)
    scaled = gn2_own * gains[1:2]
    inner = jnp.mean(scaled * mid_own, axis=1, keepdims=True)
    grad_mid = dy_own.astype(F32) + inv2_own * scaled - mid_own * (inv2_own**3 * inner)

    gm_low, far1 = join((grad_mid.astype(BF), far1))
    gm_parts = gather_rows(gm_low)
    far1 = swap(far1, "cols", 2)
    gm_parts, far1, far2 = join((gm_parts, far1, far2))

    sum1 = add_far(mine1, far1)
    far2 = swap(far2, "cols", 2)
    other1 = over(sum1)
    out_got = [swap(after(o, gm_parts[2]), "rows", k) for k, o in ((2, o2), (3, o3), (1, o1))]
    gproj, gm_all, xhat1, sent3, kernel_part, mixin_here, normed_here, wi_here = on_core(
        back_body,
        [shape((TE, 3 * W), BF), shape((T, D), BF), shape((TE, D), F32), shape((DH, 4 * W), BF), shape((3, W), F32)]
        + [shape((T, W), BF), shape((TE, D), BF), shape((D, 3 * W), BF)],
        [vmem((R, EDGE, W), F32), vmem((R, EDGE, W), F32), vmem((W, D), BF), vmem((3, W), F32)]
        + [vmem((R, mine, D), BF), vmem((TE, 3 * W), F32)],
        20,
    )((lengths,), (*gm_parts, *parts, *wo_pieces, wi_all, kernel, proj, mixin, normed1), ())
    gn1_own, t1, t2, t3, norms = on_core(
        last_body, [shape((mine, D), F32)] + [shape((mine, D), BF)] * 3 + [shape((2, D), F32)]
    )((), (), (wi_here, gproj, xhat1, norm2_part))

    t1, t2, t3, sent3, far2, other1, out_got = join((t1, t2, t3, sent3, far2, other1, out_got))
    sum2 = add_far(mine2, far2)
    (got3,) = near(sent3)
    gn1_got = [swap(t, "rows", k) for k, t in ((2, t2), (3, t3), (1, t1))]
    mine3, far3 = keep(keep3_body, (F, 4 * W), got3, normed_here, gproj, gm_all, mixin_here)
    far3 = swap(far3, "cols", 2)
    other2 = over(sum2)
    total1 = add_dp(sum1, other1)
    down_grad = total1[:F].T
    gn1_got, far3, other2, down_grad = join((gn1_got, far3, other2, down_grad))
    sum3 = add_far(mine3, far3)
    other3 = over(sum3)

    norms = after(norms, sum3)
    sends = on_core(
        finish_body, [shape((mine + Q, F), BF)] * 4, [vmem((3, mine, D), BF), vmem((3, Q, D), BF)], 6
    )((), (*gn1_got, *out_got), (gn1_own, x_own, gains, grad_mid, mid_own, out_own, norms, kernel_part))
    got = exchange([sends[order.index(k)] for k in range(C)])
    input_grad, block_output, small = on_core(
        settle_body,
        [shape((S, F), F32), shape((S, F), BF), shape((EDGE, F), F32)],
        [vmem((C, mine + Q, F), BF)],
        4,
    )((), got, ())
    more = over(small)
    if not twin:
        small = lax.psum(small, "dp")

    sum2, other2 = after((sum2, other2), got[1])
    total2 = add_dp(sum2, other2)
    gu_grad = jnp.stack([cat([total1[F:], total2[:half]], 0), total2[half:]], axis=1)
    if not twin:
        sum3 = lax.psum(sum3.astype(F32), "dp")
        other3 = sum3
    in_grad, out_grad, norm1_grad, norm2_grad, kernel_grad = on_core(
        functools.partial(total_body, twin),
        [shape((F, 3, W), F32), shape((W, F), F32)] + [shape((1, F), F32)] * 2 + [shape((3, F), F32)],
        [vmem(other3.shape, other3.dtype)],
        1,
    )((), (other3,), (sum3, small, more))
    return (
        block_output,
        input_grad,
        norm1_grad.reshape(F),
        in_grad,
        kernel_grad,
        out_grad,
        norm2_grad.reshape(F),
        gu_grad,
        down_grad,
    )


def solution(mesh):
    tok = P(("dp", "rows"), "cols")
    feat = P("cols")
    wide = P("cols", None, "rows")
    tall = P("rows", "cols")
    taps = P(None, "rows")
    return jax.shard_map(
        local,
        mesh=mesh,
        in_specs=(tok, P("dp", None), feat, wide, taps, tall, feat, wide, tall, tok),
        out_specs=(tok, tok, feat, wide, taps, tall, feat, wide, tall),
        check_vma=False,
    )
```
